32 devices in a mesh: ctx: 16 (over z, y, x), pipe: 2 (over core).
Axes of the slice: x: 2, y: 2, z: 4, core: 2. Of those that a mesh axis runs over, the one named last changes fastest.
Arguments:
- activations: float32 [2, 1, 2048, 4096], P('pipe', None, 'ctx'), may hold values from -6 to 6
- norm_gain: bfloat16 [2, 8, 4096], P('pipe', None, 'ctx'), may hold values from 0.5 to 2, as said below
- w_query: bfloat16 [2, 8, 4096, 512], P('pipe', None, 'ctx'), may hold values from -0.09375 to 0.09375
- w_keyval: bfloat16 [2, 8, 4096, 256], P('pipe', None, 'ctx'), may hold values from -0.09375 to 0.09375
- w_out: bfloat16 [2, 8, 512, 4096], P('pipe', None, None, 'ctx'), may hold values from -0.25 to 0.25
- segment_ids: int32 [1, 2048], replicated, may hold values from 0 to 3, as said below
- layer_order: int32 [2, 2], P(None, 'pipe'), may hold values from 0 to 7
Outputs:
- final_stream: float32 [2, 1, 2048, 4096], P('pipe', None, 'ctx')
The draws below stay inside these ranges and needn't reach their ends.
Inputs may be any that keep to these rules, and one draw needn't show every extreme that they name: `segment_ids`: each row never falls; every document holds 1 to 1024 positions and the last one holds exactly 1024. `norm_gain`: positive.
All inputs are finite; a program needn't handle non-finite values.
Results may differ from the reference program's by a relative error of at most 0.015.
Values may be sent and summed in bfloat16 or wider, within the bound.
A program may use at most 128 MiB of HBM per device.

```python
import math
import jax
import jax.numpy as jnp
from jax import lax

D = 4096
HEADS = 4
HD = 128
LAYERS_DEV = 8
TICKS = 2
SEQS = 1
TOK_DEV = 128
LENGTH = 2048
N_CTX = 16
N_PIPE = 2


def draw_norm_gain(key, part):
    gain_shape = (N_PIPE, LAYERS_DEV, D)
    return jnp.exp(jax.random.uniform(key, gain_shape, jnp.float32, -0.69, 0.69)).astype(jnp.bfloat16)


def draw_segment_ids(key, part):
    half = LENGTH // 2
    first_key = jax.random.fold_in(key, 11)
    second_key = jax.random.fold_in(key, 23)
    first = jax.random.randint(first_key, (SEQS, 1), 1, half - 1)
    second = first + jax.random.randint(second_key, (SEQS, 1), 1, half - first)
    places = jnp.arange(LENGTH, dtype=jnp.int32)[None, :]
    return (places >= first).astype(jnp.int32) + (places >= second).astype(jnp.int32) + (places >= half).astype(jnp.int32)


def place_ends(result, key, smallest, high):
    longest = result.shape.index(max(result.shape))
    spots = []
    for shift in (0, 1):
        where = [jax.random.randint(jax.random.fold_in(key, axis), (), 0, length) for axis, length in enumerate(result.shape)]
        where[longest] = (where[longest] + shift) % result.shape[longest]
        spots.append(tuple(where))
    return result.at[spots[0]].set(smallest).at[spots[1]].set(high)


def steps_of(rng, dims, shards, low, high):
    loudness, own = 1.0, jax.random.fold_in(rng, 6)
    for dim, parts in shards:
        draws = jnp.exp(jax.random.uniform(jax.random.fold_in(own, dim), (parts,), jnp.float32, low / len(shards), high / len(shards)))
        loudness = loudness * jnp.repeat(draws, dims[dim] // parts).reshape([-1 if axis == dim else 1 for axis in range(len(dims))])
    return loudness


def scatter_about(stream_key, shape, deviation, bound, cuts=(), kind=jnp.bfloat16):
    level = steps_of(stream_key, shape, cuts, -0.22, 0.18) if cuts else 1.0
    result = jax.random.normal(stream_key, shape, jnp.float32) * deviation * level
    return jnp.minimum(jnp.maximum(result, -bound), bound).astype(kind)


def setup_inputs(seed: int = 0) -> dict:
    splits = jax.random.split(jax.random.key(seed), 8)
    return {
        "activations": scatter_about(splits[0], (N_PIPE, SEQS, LENGTH, D), 1.0, 6.0, ((0, 2), (2, 16)), jnp.float32),
        "norm_gain": draw_norm_gain(jax.random.fold_in(splits[7], 71), 0),
        "w_query": scatter_about(splits[2], (N_PIPE, LAYERS_DEV, D, HEADS * HD), D ** -0.5, 0.09375, ((0, 2), (2, 16))),
        "w_keyval": scatter_about(splits[3], (N_PIPE, LAYERS_DEV, D, 2 * HD), D ** -0.5, 0.09375, ((0, 2), (2, 16))),
        "w_out": scatter_about(splits[4], (N_PIPE, LAYERS_DEV, HEADS * HD, D), (HEADS * HD) ** -0.5, 0.25, ((0, 2), (3, 16))),
        "segment_ids": draw_segment_ids(jax.random.fold_in(splits[7], 71), 0),
        "layer_order": place_ends(jax.random.randint(splits[6], (TICKS, N_PIPE), 0, LAYERS_DEV), jax.random.fold_in(splits[6], 1), 0, LAYERS_DEV - 1).astype(jnp.int32),
    }


def row_positions(rows):
    half = TOK_DEV // 2
    block = rows // TOK_DEV
    offset = rows % TOK_DEV
    return jnp.where(offset < half, block * half + offset, (2 * N_CTX - 1 - block) * half + offset - half).astype(jnp.int32)

def position_rows(places):
    half = TOK_DEV // 2
    block = places // half
    offset = places % half
    return jnp.where(block < N_CTX, block * TOK_DEV + offset, (2 * N_CTX - 1 - block) * TOK_DEV + half + offset).astype(jnp.int32)

def attend_sequence(query_seq, keyval_seq, segment_row):
    query_block = math.gcd(LENGTH, 1024)
    scale = 1.0 / math.sqrt(HD)
    pieces = []
    for block_index in range(LENGTH // query_block):
        first = block_index * query_block
        last = first + query_block
        query_part = query_seq[first:last].astype(jnp.float32)
        key_part = keyval_seq[:last, :HD].astype(jnp.float32)
        value_part = keyval_seq[:last, HD:].astype(jnp.float32)
        scores = jnp.einsum('qhd,kd->hqk', query_part, key_part) * scale
        query_pos = jnp.arange(first, last, dtype=jnp.int32)
        key_pos = jnp.arange(last, dtype=jnp.int32)
        allowed = (key_pos[None, :] <= query_pos[:, None]) & (segment_row[None, :last] == segment_row[first:last, None])
        scores = jnp.where(allowed[None], scores, -1e+30)
        row_max = lax.optimization_barrier(jnp.max(scores, axis=-1, keepdims=True))
        probs = jnp.where(allowed[None], jnp.exp(scores - row_max), 0.0)
        totals = lax.optimization_barrier(jnp.sum(probs, axis=-1))
        probs_low = lax.optimization_barrier(probs.astype(jnp.bfloat16))
        summed = jnp.einsum('hqk,kd->qhd', probs_low.astype(jnp.float32), value_part)
        pieces.append((summed / jnp.transpose(totals)[:, :, None]).astype(jnp.bfloat16))
    return jnp.concatenate(pieces, axis=0)

def layer_apply(stream, gain_row, query_weight, keyval_weight, out_weight, segment_ids):
    stream_f = stream.astype(jnp.float32)
    mean_square = lax.optimization_barrier(jnp.mean(stream_f * stream_f, axis=-1, keepdims=True))
    normed = (stream_f * lax.rsqrt(mean_square + 1e-05) * gain_row.astype(jnp.float32)).astype(jnp.bfloat16)
    flat = normed.reshape(SEQS * LENGTH, D)
    queries = jnp.dot(flat, query_weight, preferred_element_type=jnp.float32).astype(jnp.bfloat16)
    queries = queries.reshape(SEQS, LENGTH, HEADS, HD)
    keyvals = jnp.dot(flat, keyval_weight, preferred_element_type=jnp.float32).astype(jnp.bfloat16)
    keyvals = keyvals.reshape(SEQS, LENGTH, 2 * HD)
    places = jnp.arange(LENGTH, dtype=jnp.int32)
    by_position = position_rows(places)
    by_row = row_positions(places)
    queries = jnp.take(queries, by_position, axis=1)
    keyvals = jnp.take(keyvals, by_position, axis=1)

    def one_sequence(packed):
        query_seq, keyval_seq, segment_row = packed
        return attend_sequence(query_seq, keyval_seq, segment_row)
    attended = lax.map(one_sequence, (queries, keyvals, segment_ids))
    attended = jnp.take(attended, by_row, axis=1)
    attended = attended.reshape(SEQS * LENGTH, HEADS * HD)
    mixed = jnp.dot(attended, out_weight, preferred_element_type=jnp.float32)
    return stream_f + mixed.reshape(SEQS, LENGTH, D)

def reference(activations, norm_gain, w_query, w_keyval, w_out, segment_ids, layer_order):
    batches = [activations[index] for index in range(N_PIPE)]
    for tick_index in range(TICKS):
        for index in range(N_PIPE):
            section = (index + tick_index) % N_PIPE
            layer = layer_order[tick_index, section]
            batches[index] = layer_apply(batches[index], norm_gain[section, layer], w_query[section, layer], w_keyval[section, layer], w_out[section, layer], segment_ids)
    return jnp.stack([batches[(place - TICKS) % N_PIPE] for place in range(N_PIPE)])
```

```python
import functools
import itertools
import math

import jax
import jax.numpy as jnp
from jax import lax
from jax.experimental import pallas as pl
from jax.experimental.pallas import tpu as pltpu
from jax.sharding import PartitionSpec as P

TICKS = 2
HALVES = 2
MESH = pl.DeviceIdType.MESH
LOW = jnp.bfloat16
FULL = jnp.float32


def grid_of(count):
    known = {
        16: ((2, 2, 2, 2), (1, 3), (0, 2), (0, 1), (2, 3)),
        32: ((4, 8), (0,), (1,), (0,), (1,)),
    }
    return known[count]


class Grid:
    def __init__(self, count):
        self.sizes, self.split_dims, self.share_dims, self.major_dims, self.minor_dims = grid_of(count)
        self.rank = len(self.sizes)
        self.strides = [math.prod(self.sizes[d + 1 :]) for d in range(self.rank)]
        self.split = self.deltas(self.split_dims)
        self.share = self.deltas(self.share_dims)
        self.major = self.deltas(self.major_dims)
        self.minor = self.deltas(self.minor_dims)
        self.hops = [
            self.along(d, by) for d in self.share_dims for by in range(1, self.sizes[d])
        ]
        self.zero = (0,) * self.rank

    def deltas(self, dims):
        ranges = [range(self.sizes[d]) if d in dims else range(1) for d in range(self.rank)]
        return list(itertools.product(*ranges))

    def along(self, dim, by):
        return tuple(by if d == dim else 0 for d in range(self.rank))

    def flat(self, delta):
        return sum(delta[d] * self.strides[d] for d in range(self.rank))

    def minus(self, one, other):
        return tuple((a - b) % s for a, b, s in zip(one, other, self.sizes))

    def plus(self, one, other):
        return tuple((a + b) % s for a, b, s in zip(one, other, self.sizes))

    def within(self, coords, dims):
        total = 0
        for d in dims:
            total = total * self.sizes[d] + coords[d]
        return total


def layers_kernel(grid, *refs):
    order, stream_hbm, gain_hbm, query_hbm, keyval_hbm, out_hbm, segments = refs[:7]
    result = refs[7]
    (
        stream,
        gains,
        query_all,
        keyval_all,
        out_all,
        sent,
        kept,
        next_kept,
        first_sum,
        w_keyval,
        w_query,
        w_out,
        later_keyval,
        later_query,
        later_out,
        part_keyval,
        part_query,
        came_keyval,
        came_query,
        part_square,
        came_square,
        keyvals,
        attended,
        back,
        came_back,
        bias,
        load_sems,
        x_send,
        x_recv,
        w_send,
        w_recv,
        pk_send,
        pk_recv,
        pq_send,
        pq_recv,
        sq_send,
        sq_recv,
        kv_send,
        kv_recv,
        at_send,
        at_recv,
        b_send,
        b_recv,
    ) = refs[8:]
    sizes = grid.sizes
    ctx_count = math.prod(sizes)
    me = lax.axis_index("ctx")
    section = lax.axis_index("pipe")
    pipe_count = lax.axis_size("pipe")
    coords = [(me // grid.strides[d]) % sizes[d] for d in range(grid.rank)]
    split_count, share_count = len(grid.split), len(grid.share)
    tok_rows, model_width = stream.shape
    half = tok_rows // HALVES
    block = model_width // ctx_count
    wide = block * share_count
    query_width = w_query.shape[-1]
    kv_width = w_keyval.shape[-1]
    head_dim = kv_width // 2
    head_count = query_width // head_dim
    scale = 1.0 / math.sqrt(head_dim)
    stacked = split_count * half

    def moved(delta):
        return [(coords[d] + delta[d]) % sizes[d] for d in range(grid.rank)]

    def place(delta):
        return sum(c * s for c, s in zip(moved(delta), grid.strides))

    def split_slot(delta):
        return grid.within(moved(delta), grid.split_dims)

    def share_slot(delta):
        return grid.within(moved(delta), grid.share_dims)

    def rank_of(half_index, delta):
        where = place(delta)
        return where if half_index == 0 else ctx_count - 1 - where

    def columns(index):
        return pl.ds(pl.multiple_of(index * block, block), block)

    def rows(half_index):
        return pl.ds(half_index * half, half)

    finish = []

    def remote(src, dst, send, recv, ctx, pipe=None):
        device = {"ctx": ctx} if pipe is None else {"ctx": ctx, "pipe": pipe}
        return pltpu.make_async_remote_copy(
            src_ref=src,
            dst_ref=dst,
            send_sem=send,
            recv_sem=recv,
            device_id=device,
            device_id_type=MESH,
        )

    def push(copy, when=None):
        if when is None:
            copy.start()
        else:
            pl.when(when)(copy.start)
        finish.append((copy, when))

    loads = []

    def load(src, dst):
        copy = pltpu.make_async_copy(src, dst, load_sems.at[len(loads)])
        copy.start()
        loads.append(copy)
        return copy

    load_stream = [load(stream_hbm.at[rows(h)], stream.at[rows(h)]) for h in range(HALVES)]
    load_gain = load(gain_hbm, gains)
    load_keyval = load(keyval_hbm, keyval_all)
    load_query = load(query_hbm, query_all)
    load_out = load(out_hbm, out_all)

    keyvals[...] = jnp.zeros_like(keyvals)

    near = sorted(
        set(grid.split + grid.hops + grid.major + grid.minor) - {grid.zero}
    )
    barrier = pltpu.get_barrier_semaphore()
    greeted = 0
    for delta in near:
        pl.semaphore_signal(
            barrier, inc=1, device_id={"ctx": place(delta)}, device_id_type=MESH
        )
        greeted += 1
    for by in sorted({1, pipe_count - 1}):
        for delta in [grid.zero] + grid.hops:
            pl.semaphore_signal(
                barrier,
                inc=1,
                device_id={"ctx": place(delta), "pipe": (section + by) % pipe_count},
                device_id_type=MESH,
            )
            greeted += 1

    key_rel = lax.broadcasted_iota(jnp.int32, (half, ctx_count * half), 1)
    row_rel = lax.broadcasted_iota(jnp.int32, (half, ctx_count * half), 0)
    for h in range(HALVES):
        query_rel = row_rel + rank_of(h, grid.zero) * half
        seg = segments[:, h * ctx_count * half : (h + 1) * ctx_count * half].astype(FULL)
        seg = jnp.broadcast_to(seg, (half, ctx_count * half))
        own = jnp.sum(jnp.where(key_rel == query_rel, seg, 0.0), axis=1, keepdims=True)
        bias[h] = jnp.where((key_rel <= query_rel) & (seg == own), 0.0, -1e30)

    pl.semaphore_wait(barrier, greeted)

    others = [delta for delta in grid.split if delta != grid.zero]
    factors = {}

    def send_stream(h):
        load_stream[h].wait()
        squares = jnp.zeros((half, 1), FULL)
        for index, delta in enumerate(grid.split):
            target = kept.at[h, split_slot(grid.zero)] if delta == grid.zero else sent.at[h, index]
            for s, share in enumerate(grid.share):
                where = grid.plus(delta, share)
                value = stream[rows(h), columns(place(where))]
                squares += jnp.sum(value * value, axis=1, keepdims=True)
                target[:, columns(share_slot(share))] = value.astype(LOW)
            if delta != grid.zero:
                seen = grid.split.index(grid.minus(grid.zero, delta))
                push(
                    remote(
                        sent.at[h, index],
                        kept.at[h, split_slot(grid.zero)],
                        x_send.at[h, index],
                        x_recv.at[h, seen],
                        place(delta),
                    )
                )
        factors[0, h] = lax.rsqrt(squares / model_width + 1e-05)

    def take_stream(h):
        for index, delta in enumerate(grid.split):
            if delta != grid.zero:
                landing = kept.at[h, split_slot(delta)]
                remote(
                    landing, landing, x_send.at[h, index], x_recv.at[h, index], place(delta)
                ).wait_recv()

    wholes = [w_keyval, w_query, w_out]
    laters = [later_keyval, later_query, later_out]
    used = {}

    def fill(kind, tick):
        layer = order[tick, 0]
        source = [keyval_all, query_all, out_all][kind]
        value = source[layer]
        if kind < 2:
            level = lax.broadcasted_iota(jnp.int32, gains.shape, 0)
            gain = jnp.where(level == layer, gains[...].astype(FULL), 0.0)
            gain = jnp.sum(gain, axis=0, keepdims=True)
            gain = jnp.transpose(jnp.broadcast_to(gain, (128, block)))
            value = value.astype(FULL)
            value = jnp.concatenate(
                [value[:, c : c + 128] * gain for c in range(0, value.shape[1], 128)], axis=1
            ).astype(LOW)
        if tick == 0:
            wholes[kind][tick, share_slot(grid.zero)] = value
        else:
            laters[kind][...] = value

    def next_send(kind, tick):
        count = used.get((kind, tick), 0)
        used[kind, tick] = count + 1
        return w_send.at[kind, tick, count]

    def begin(kind, tick):
        slot = share_slot(grid.zero)
        landing = wholes[kind].at[tick, slot]
        source = landing if tick == 0 else laters[kind]
        pipe = None if tick == 0 else (section + pipe_count - tick) % pipe_count
        for delta in grid.hops:
            seen = grid.share.index(grid.minus(grid.zero, delta))
            push(
                remote(
                    source,
                    landing,
                    next_send(kind, tick),
                    w_recv.at[kind, tick, seen],
                    place(delta),
                    pipe,
                )
            )
        if tick:
            push(
                remote(
                    source,
                    landing,
                    next_send(kind, tick),
                    w_recv.at[kind, tick, 0],
                    me,
                    pipe,
                )
            )

    def take_weight(kind, tick, phase):
        dims = grid.share_dims
        if phase == 0 and tick:
            landing = wholes[kind].at[tick, share_slot(grid.zero)]
            remote(
                landing,
                landing,
                w_send.at[kind, tick, 0],
                w_recv.at[kind, tick, 0],
                me,
                (section + pipe_count - tick) % pipe_count,
            ).wait_recv()
        for delta in grid.share:
            if delta[dims[phase]] == 0 or any(delta[d] for d in dims[phase + 1 :]):
                continue
            landing = wholes[kind].at[tick, share_slot(delta)]
            remote(
                landing,
                landing,
                w_send.at[kind, tick, 0],
                w_recv.at[kind, tick, grid.share.index(delta)],
                place(grid.along(dims[phase], 1)),
            ).wait_recv()
            for dim in dims[phase + 1 :]:
                for by in range(1, sizes[dim]):
                    hop = grid.along(dim, by)
                    seen = grid.share.index(grid.minus(delta, hop))
                    push(
                        remote(
                            landing,
                            landing,
                            next_send(kind, tick),
                            w_recv.at[kind, tick, seen],
                            place(hop),
                        )
                    )

    phases = range(len(grid.share_dims))
    layered = [kept, next_kept]

    def project(kind, tick, h):
        part = [part_keyval, part_query][kind]
        came = [came_keyval, came_query][kind]
        send, recv = [(pk_send, pk_recv), (pq_send, pq_recv)][kind]
        width = part.shape[-1]
        value = layered[tick][h].reshape(stacked, wide)
        weight = wholes[kind][tick].reshape(wide, width)
        total = jnp.dot(value, weight, preferred_element_type=FULL).astype(LOW)
        part[tick, h] = total.reshape(split_count, half, width)
        for index, delta in enumerate(grid.split):
            if delta != grid.zero:
                seen = grid.split.index(grid.minus(grid.zero, delta))
                push(
                    remote(
                        part.at[tick, h, split_slot(delta)],
                        came.at[tick, h, seen],
                        send.at[tick, h, index],
                        recv.at[tick, h, seen],
                        place(delta),
                    )
                )

    def summed(kind, tick, h):
        part = [part_keyval, part_query][kind]
        came = [came_keyval, came_query][kind]
        send, recv = [(pk_send, pk_recv), (pq_send, pq_recv)][kind]
        total = part[tick, h, split_slot(grid.zero)].astype(FULL)
        for index, delta in enumerate(grid.split):
            if delta != grid.zero:
                landing = came.at[tick, h, index]
                remote(
                    landing,
                    landing,
                    send.at[tick, h, index],
                    recv.at[tick, h, index],
                    place(delta),
                ).wait_recv()
                total += came[tick, h, index].astype(FULL)
        return (total * factors[tick, h]).astype(LOW)

    def send_squares(h, total):
        ones = jnp.ones((8, 128), FULL)
        for index, delta in enumerate(grid.split):
            piece = total[index * half : (index + 1) * half]
            piece = jnp.concatenate([piece] * (128 // half), axis=0)
            part_square[h, index] = lax.dot_general(
                ones,
                piece,
                (((1,), (1,)), ((), ())),
                preferred_element_type=FULL,
                precision=lax.Precision.HIGHEST,
            )
        for index, delta in enumerate(grid.split):
            if delta != grid.zero:
                seen = grid.split.index(grid.minus(grid.zero, delta))
                push(
                    remote(
                        part_square.at[h, split_slot(delta)],
                        came_square.at[h, seen],
                        sq_send.at[h, index],
                        sq_recv.at[h, seen],
                        place(delta),
                    )
                )

    def take_squares(h):
        total = part_square[h, split_slot(grid.zero)]
        for index, delta in enumerate(grid.split):
            if delta != grid.zero:
                landing = came_square.at[h, index]
                remote(
                    landing, landing, sq_send.at[h, index], sq_recv.at[h, index], place(delta)
                ).wait_recv()
                total += came_square[h, index]
        column = jnp.transpose(total)[:half, 0:1]
        factors[1, h] = lax.rsqrt(column / model_width + 1e-05)

    def before(h, delta):
        theirs = grid.within(moved(delta), grid.major_dims)
        ours = grid.within(coords, grid.major_dims)
        return theirs < ours if h == 0 else theirs > ours

    def after(h, delta):
        theirs = grid.within(moved(delta), grid.major_dims)
        ours = grid.within(coords, grid.major_dims)
        return theirs > ours if h == 0 else theirs < ours

    def relay(tick, h, delta, hop, when):
        landing = keyvals.at[tick, h, rank_of(h, delta)]
        seen = grid.minus(delta, hop)
        push(
            remote(
                landing,
                landing,
                kv_send.at[tick, h, grid.flat(grid.plus(delta, hop))],
                kv_recv.at[tick, h, grid.flat(seen)],
                place(hop),
            ),
            when,
        )

    def send_keyvals(tick, h):
        keyvals[tick, h, rank_of(h, grid.zero)] = summed(0, tick, h)
        for delta in grid.major:
            if delta != grid.zero:
                relay(tick, h, grid.zero, delta, after(h, delta))
        for hop in grid.minor:
            if hop != grid.zero:
                relay(tick, h, grid.zero, hop, None)

    def wait_keyvals(tick, h, delta):
        landing = keyvals.at[tick, h, rank_of(h, delta)]
        remote(
            landing,
            landing,
            kv_send.at[tick, h, 0],
            kv_recv.at[tick, h, grid.flat(delta)],
            place(grid.along(0, 1)),
        ).wait_recv()

    def pass_keyvals(tick, h):
        for delta in grid.major:
            if delta != grid.zero:
                when = before(h, delta)
                pl.when(when)(functools.partial(wait_keyvals, tick, h, delta))
                for hop in grid.minor:
                    if hop != grid.zero:
                        relay(tick, h, delta, hop, when)

    def take_keyvals(tick, h):
        for hop in grid.minor:
            if hop != grid.zero:
                wait_keyvals(tick, h, hop)
        for delta in grid.major:
            if delta != grid.zero:

                @pl.when(before(h, delta))
                def _(delta=delta):
                    for hop in grid.minor:
                        if hop != grid.zero:
                            wait_keyvals(tick, h, grid.plus(delta, hop))

    def attend(tick, h):
        query = summed(1, tick, h)
        query = jnp.concatenate(
            [query[:, i * head_dim : (i + 1) * head_dim] for i in range(head_count)], axis=0
        )
        take_keyvals(tick, h)
        keys = keyvals[tick, h, :, :, :head_dim].reshape(ctx_count * half, head_dim)
        values = keyvals[tick, h, :, :, head_dim:].reshape(ctx_count * half, head_dim)
        scores = lax.dot_general(
            query, keys, (((1,), (1,)), ((), ())), preferred_element_type=FULL
        )
        scores = scores.reshape(head_count, half, ctx_count * half) * scale + bias[h][None]
        probs = jnp.exp(scores - jnp.max(scores, axis=-1, keepdims=True))
        totals = jnp.sum(probs, axis=-1, keepdims=True)
        mixed = jnp.dot(
            probs.astype(LOW).reshape(head_count * half, ctx_count * half),
            values,
            preferred_element_type=FULL,
        ).reshape(head_count, half, head_dim)
        mixed = (mixed / totals).astype(LOW)
        own = attended.at[tick, h, split_slot(grid.zero)]
        for i in range(head_count):
            own[:, i * head_dim : (i + 1) * head_dim] = mixed[i]
        for index, delta in enumerate(grid.split):
            if delta != grid.zero:
                seen = grid.split.index(grid.minus(grid.zero, delta))
                push(
                    remote(
                        own,
                        own,
                        at_send.at[tick, h, index],
                        at_recv.at[tick, h, seen],
                        place(delta),
                    )
                )

    def take_attended(tick, h):
        for index, delta in enumerate(grid.split):
            if delta != grid.zero:
                landing = attended.at[tick, h, split_slot(delta)]
                remote(
                    landing,
                    landing,
                    at_send.at[tick, h, index],
                    at_recv.at[tick, h, index],
                    place(delta),
                ).wait_recv()

    def mix_first(h):
        take_attended(0, h)
        value = attended[0, h].reshape(stacked, query_width)
        squares = jnp.zeros((stacked, 128), FULL)
        for s in range(share_count):
            cols = pl.ds(s * block, block)
            mixed = jnp.dot(value, w_out[0, s], preferred_element_type=FULL)
            first_sum[h, :, :, cols] = mixed.reshape(split_count, half, block)
            following = kept[h, :, :, cols].reshape(stacked, block).astype(FULL) + mixed
            next_kept[h, :, :, cols] = following.astype(LOW).reshape(split_count, half, block)
            following = following * following
            for c in range(0, block, 128):
                squares += following[:, c : c + 128]
        send_squares(h, squares)

    def mix_last(h):
        take_attended(1, h)
        value = attended[1, h].reshape(stacked, query_width)
        for s in range(share_count):
            cols = pl.ds(s * block, block)
            mixed = jnp.dot(value, w_out[1, s], preferred_element_type=FULL)
            mixed = mixed.reshape(split_count, half, block) + first_sum[h, :, :, cols]
            back[h, :, :, cols] = mixed.astype(LOW)
        for index, delta in enumerate(grid.split):
            if delta != grid.zero:
                seen = grid.split.index(grid.minus(grid.zero, delta))
                push(
                    remote(
                        back.at[h, split_slot(delta)],
                        came_back.at[h, seen],
                        b_send.at[h, index],
                        b_recv.at[h, seen],
                        place(delta),
                    )
                )

    def end(h):
        for index, delta in enumerate(grid.split):
            if delta == grid.zero:
                source = back.at[h, split_slot(grid.zero)]
            else:
                source = came_back.at[h, index]
                remote(
                    source, source, b_send.at[h, index], b_recv.at[h, index], place(delta)
                ).wait_recv()
            for share in grid.share:
                cols = columns(place(grid.plus(delta, share)))
                value = source[:, columns(share_slot(share))].astype(FULL)
                result[rows(h), cols] = stream[rows(h), cols] + value

    halves = range(HALVES)
    send_stream(0)
    load_gain.wait()
    load_keyval.wait()
    fill(0, 0)
    begin(0, 0)
    send_stream(1)
    load_query.wait()
    fill(1, 0)
    begin(1, 0)
    load_out.wait()
    fill(2, 0)
    begin(2, 0)
    for kind in range(3):
        fill(kind, 1)
    for phase in phases:
        take_weight(0, 0, phase)
    for h in halves:
        take_stream(h)
        project(0, 0, h)
    for h in halves:
        send_keyvals(0, h)
    take_weight(1, 0, 0)
    for h in halves:
        pass_keyvals(0, h)
    for phase in phases[1:]:
        take_weight(1, 0, phase)
    for h in halves:
        project(1, 0, h)
    begin(0, 1)
    begin(1, 1)
    take_weight(2, 0, 0)
    for h in halves:
        attend(0, h)
    for phase in phases[1:]:
        take_weight(2, 0, phase)
    begin(2, 1)
    take_weight(0, 1, 0)
    mix_first(0)
    for phase in phases[1:]:
        take_weight(0, 1, phase)
    project(0, 1, 0)
    mix_first(1)
    project(0, 1, 1)
    for h in halves:
        take_squares(h)
        send_keyvals(1, h)
    take_weight(1, 1, 0)
    for h in halves:
        pass_keyvals(1, h)
    for phase in phases[1:]:
        take_weight(1, 1, phase)
    for h in halves:
        project(1, 1, h)
    take_weight(2, 1, 0)
    for h in halves:
        attend(1, h)
    for phase in phases[1:]:
        take_weight(2, 1, phase)
    for h in halves:
        mix_last(h)
    for h in halves:
        end(h)
    for copy, when in finish:
        if when is None:
            copy.wait_send()
        else:
            pl.when(when)(copy.wait_send)


def run_layers(order, stream, gain, query, keyval, out, segments, ctx_count):
    grid = Grid(ctx_count)
    split, share = len(grid.split), len(grid.share)
    tok_rows, model_width = stream.shape
    half = tok_rows // HALVES
    block = model_width // ctx_count
    wide = block * share
    query_width, kv_width = query.shape[-1], keyval.shape[-1]
    vmem = pl.BlockSpec(memory_space=pltpu.VMEM)
    hbm = pl.BlockSpec(memory_space=pl.ANY)
    smem = pl.BlockSpec(memory_space=pltpu.SMEM)
    dma = pltpu.SemaphoreType.DMA
    scratch = [
        pltpu.VMEM(stream.shape, FULL),
        pltpu.VMEM(gain.shape, LOW),
        pltpu.VMEM(query.shape, LOW),
        pltpu.VMEM(keyval.shape, LOW),
        pltpu.VMEM(out.shape, LOW),
        pltpu.VMEM((HALVES, split, half, wide), LOW),
        pltpu.VMEM((HALVES, split, half, wide), LOW),
        pltpu.VMEM((HALVES, split, half, wide), LOW),
        pltpu.VMEM((HALVES, split, half, wide), FULL),
        pltpu.VMEM((TICKS, share, block, kv_width), LOW),
        pltpu.VMEM((TICKS, share, block, query_width), LOW),
        pltpu.VMEM((TICKS, share, query_width, block), LOW),
        pltpu.VMEM((block, kv_width), LOW),
        pltpu.VMEM((block, query_width), LOW),
        pltpu.VMEM((query_width, block), LOW),
        pltpu.VMEM((TICKS, HALVES, split, half, kv_width), LOW),
        pltpu.VMEM((TICKS, HALVES, split, half, query_width), LOW),
        pltpu.VMEM((TICKS, HALVES, split, half, kv_width), LOW),
        pltpu.VMEM((TICKS, HALVES, split, half, query_width), LOW),
        pltpu.VMEM((HALVES, split, 8, 128), FULL),
        pltpu.VMEM((HALVES, split, 8, 128), FULL),
        pltpu.VMEM((TICKS, HALVES, ctx_count, half, kv_width), LOW),
        pltpu.VMEM((TICKS, HALVES, split, half, query_width), LOW),
        pltpu.VMEM((HALVES, split, half, wide), LOW),
        pltpu.VMEM((HALVES, split, half, wide), LOW),
        pltpu.VMEM((HALVES, half, ctx_count * half), FULL),
        dma((8,)),
        dma((HALVES, split)),
        dma((HALVES, split)),
        dma((3, TICKS, share + 2)),
        dma((3, TICKS, share)),
    ]
    scratch += [dma((TICKS, HALVES, split))] * 4
    scratch += [dma((HALVES, split))] * 2
    scratch += [dma((TICKS, HALVES, ctx_count))] * 2
    scratch += [dma((TICKS, HALVES, split))] * 2
    scratch += [dma((HALVES, split))] * 2
    return pl.pallas_call(
        functools.partial(layers_kernel, grid),
        out_shape=jax.ShapeDtypeStruct(stream.shape, FULL),
        in_specs=[smem] + [hbm] * 5 + [vmem],
        out_specs=vmem,
        scratch_shapes=scratch,
        compiler_params=pltpu.CompilerParams(
            collective_id=0, has_side_effects=True, vmem_limit_bytes=56 * 1024 * 1024
        ),
    )(order, stream, gain, query, keyval, out, segments)


def body(activations, norm_gain, w_query, w_keyval, w_out, segment_ids, layer_order):
    ctx_count = lax.axis_size("ctx")
    pipe_count = lax.axis_size("pipe")
    state = run_layers(
        layer_order,
        activations[0, 0],
        norm_gain[0],
        w_query[0],
        w_keyval[0],
        w_out[0],
        segment_ids,
        ctx_count,
    )
    if TICKS % pipe_count:
        pairs = [(i, (i + TICKS) % pipe_count) for i in range(pipe_count)]
        state = lax.ppermute(state, "pipe", pairs)
    return state[None, None]


def solution(mesh):
    in_specs = (
        P("pipe", None, "ctx", None),
        P("pipe", None, "ctx"),
        P("pipe", None, "ctx", None),
        P("pipe", None, "ctx", None),
        P("pipe", None, None, "ctx"),
        P(),
        P(None, "pipe"),
    )
    out_specs = P("pipe", None, "ctx", None)
    return jax.shard_map(body, mesh=mesh, in_specs=in_specs, out_specs=out_specs, check_vma=False)
```

```python
import functools
import itertools
import math

import jax
import jax.numpy as jnp
from jax import lax
from jax.experimental import pallas as pl
from jax.experimental.pallas import tpu as pltpu
from jax.sharding import PartitionSpec as P

TICKS = 2
HALVES = 2
MESH = pl.DeviceIdType.MESH
LOW = jnp.bfloat16
FULL = jnp.float32


def grid_of(count):
    known = {
        16: ((2, 2, 2, 2), (1, 3), (0, 2), (0, 1), (2, 3)),
        32: ((4, 8), (0,), (1,), (0,), (1,)),
    }
    return known[count]


class Grid:
    def __init__(self, count):
        self.sizes, self.split_dims, self.share_dims, self.major_dims, self.minor_dims = grid_of(count)
        self.rank = len(self.sizes)
        self.strides = [math.prod(self.sizes[d + 1 :]) for d in range(self.rank)]
        self.split = self.deltas(self.split_dims)
        self.share = self.deltas(self.share_dims)
        self.major = self.deltas(self.major_dims)
        self.minor = self.deltas(self.minor_dims)
        self.hops = [
            self.along(d, by) for d in self.share_dims for by in range(1, self.sizes[d])
        ]
        self.zero = (0,) * self.rank

    def deltas(self, dims):
        ranges = [range(self.sizes[d]) if d in dims else range(1) for d in range(self.rank)]
        return list(itertools.product(*ranges))

    def along(self, dim, by):
        return tuple(by if d == dim else 0 for d in range(self.rank))

    def flat(self, delta):
        return sum(delta[d] * self.strides[d] for d in range(self.rank))

    def minus(self, one, other):
        return tuple((a - b) % s for a, b, s in zip(one, other, self.sizes))

    def plus(self, one, other):
        return tuple((a + b) % s for a, b, s in zip(one, other, self.sizes))

    def within(self, coords, dims):
        total = 0
        for d in dims:
            total = total * self.sizes[d] + coords[d]
        return total


def layers_kernel(grid, *refs):
    order, stream_hbm, gain_hbm, query_hbm, keyval_hbm, out_hbm, segments = refs[:7]
    result = refs[7]
    (
        stream,
        gains,
        query_all,
        keyval_all,
        out_all,
        sent,
        kept,
        next_kept,
        first_sum,
        w_keyval,
        w_query,
        w_out,
        later_keyval,
        later_query,
        later_out,
        part_keyval,
        part_query,
        came_keyval,
        came_query,
        part_square,
        came_square,
        keyvals,
        attended,
        back,
        came_back,
        bias,
        load_sems,
        x_send,
        x_recv,
        w_send,
        w_recv,
        pk_send,
        pk_recv,
        pq_send,
        pq_recv,
        sq_send,
        sq_recv,
        kv_send,
        kv_recv,
        at_send,
        at_recv,
        b_send,
        b_recv,
    ) = refs[8:]
    sizes = grid.sizes
    ctx_count = math.prod(sizes)
    me = lax.axis_index("ctx")
    section = lax.axis_index("pipe")
    pipe_count = lax.axis_size("pipe")
    coords = [(me // grid.strides[d]) % sizes[d] for d in range(grid.rank)]
    split_count, share_count = len(grid.split), len(grid.share)
    tok_rows, model_width = stream.shape
    half = tok_rows // HALVES
    block = model_width // ctx_count
    wide = block * share_count
    query_width = w_query.shape[-1]
    kv_width = w_keyval.shape[-1]
    head_dim = kv_width // 2
    head_count = query_width // head_dim
    scale = 1.0 / math.sqrt(head_dim)
    stacked = split_count * half

    def moved(delta):
        return [(coords[d] + delta[d]) % sizes[d] for d in range(grid.rank)]

    def place(delta):
        return sum(c * s for c, s in zip(moved(delta), grid.strides))

    def split_slot(delta):
        return grid.within(moved(delta), grid.split_dims)

    def share_slot(delta):
        return grid.within(moved(delta), grid.share_dims)

    def rank_of(half_index, delta):
        where = place(delta)
        return where if half_index == 0 else ctx_count - 1 - where

    def columns(index):
        return pl.ds(pl.multiple_of(index * block, block), block)

    def rows(half_index):
        return pl.ds(half_index * half, half)

    finish = []

    def remote(src, dst, send, recv, ctx, pipe=None):
        device = {"ctx": ctx} if pipe is None else {"ctx": ctx, "pipe": pipe}
        return pltpu.make_async_remote_copy(
            src_ref=src,
            dst_ref=dst,
            send_sem=send,
            recv_sem=recv,
            device_id=device,
            device_id_type=MESH,
        )

    def push(copy, when=None):
        if when is None:
            copy.start()
        else:
            pl.when(when)(copy.start)
        finish.append((copy, when))

    loads = []

    def load(src, dst):
        copy = pltpu.make_async_copy(src, dst, load_sems.at[len(loads)])
        copy.start()
        loads.append(copy)
        return copy

    load_stream = [load(stream_hbm.at[rows(h)], stream.at[rows(h)]) for h in range(HALVES)]
    load_gain = load(gain_hbm, gains)
    load_keyval = load(keyval_hbm, keyval_all)
    load_query = load(query_hbm, query_all)
    load_out = load(out_hbm, out_all)

    keyvals[...] = jnp.zeros_like(keyvals)

    near = sorted(
        set(grid.split + grid.hops + grid.major + grid.minor) - {grid.zero}
    )
    barrier = pltpu.get_barrier_semaphore()
    greeted = 0
    for delta in near:
        pl.semaphore_signal(
            barrier, inc=1, device_id={"ctx": place(delta)}, device_id_type=MESH
        )
        greeted += 1
    for by in sorted({1, pipe_count - 1}):
        for delta in [grid.zero] + grid.hops:
            pl.semaphore_signal(
                barrier,
                inc=1,
                device_id={"ctx": place(delta), "pipe": (section + by) % pipe_count},
                device_id_type=MESH,
            )
            greeted += 1

    key_rel = lax.broadcasted_iota(jnp.int32, (half, ctx_count * half), 1)
    row_rel = lax.broadcasted_iota(jnp.int32, (half, ctx_count * half), 0)
    for h in range(HALVES):
        query_rel = row_rel + rank_of(h, grid.zero) * half
        seg = segments[:, h * ctx_count * half : (h + 1) * ctx_count * half].astype(FULL)
        seg = jnp.broadcast_to(seg, (half, ctx_count * half))
        own = jnp.sum(jnp.where(key_rel == query_rel, seg, 0.0), axis=1, keepdims=True)
        bias[h] = jnp.where((key_rel <= query_rel) & (seg == own), 0.0, -1e30)

    pl.semaphore_wait(barrier, greeted)

    others = [delta for delta in grid.split if delta != grid.zero]
    factors = {}

    def send_stream(h):
        load_stream[h].wait()
        squares = jnp.zeros((half, 1), FULL)
        for index, delta in enumerate(grid.split):
            target = kept.at[h, split_slot(grid.zero)] if delta == grid.zero else sent.at[h, index]
            for s, share in enumerate(grid.share):
                where = grid.plus(delta, share)
                value = stream[rows(h), columns(place(where))]
                squares += jnp.sum(value * value, axis=1, keepdims=True)
                target[:, columns(share_slot(share))] = value.astype(LOW)
            if delta != grid.zero:
                seen = grid.split.index(grid.minus(grid.zero, delta))
                push(
                    remote(
                        sent.at[h, index],
                        kept.at[h, split_slot(grid.zero)],
                        x_send.at[h, index],
                        x_recv.at[h, seen],
                        place(delta),
                    )
                )
        factors[0, h] = lax.rsqrt(squares / model_width + 1e-05)

    def take_stream(h):
        for index, delta in enumerate(grid.split):
            if delta != grid.zero:
                landing = kept.at[h, split_slot(delta)]
                remote(
                    landing, landing, x_send.at[h, index], x_recv.at[h, index], place(delta)
                ).wait_recv()

    wholes = [w_keyval, w_query, w_out]
    laters = [later_keyval, later_query, later_out]
    used = {}

    def fill(kind, tick):
        layer = order[0, tick]
        source = [keyval_all, query_all, out_all][kind]
        value = source[layer]
        if kind < 2:
            level = lax.broadcasted_iota(jnp.int32, gains.shape, 0)
            gain = jnp.where(level == layer, gains[...].astype(FULL), 0.0)
            gain = jnp.sum(gain, axis=0, keepdims=True)
            gain = jnp.transpose(jnp.broadcast_to(gain, (128, block)))
            value = value.astype(FULL)
            value = jnp.concatenate(
                [value[:, c : c + 128] * gain for c in range(0, value.shape[1], 128)], axis=1
            ).astype(LOW)
        if tick == 0:
            wholes[kind][tick, share_slot(grid.zero)] = value
        else:
            laters[kind][...] = value

    def next_send(kind, tick):
        count = used.get((kind, tick), 0)
        used[kind, tick] = count + 1
        return w_send.at[kind, tick, count]

    def begin(kind, tick):
        slot = share_slot(grid.zero)
        landing = wholes[kind].at[tick, slot]
        source = landing if tick == 0 else laters[kind]
        pipe = None if tick == 0 else (section + pipe_count - tick) % pipe_count
        for delta in grid.hops:
            seen = grid.share.index(grid.minus(grid.zero, delta))
            push(
                remote(
                    source,
                    landing,
                    next_send(kind, tick),
                    w_recv.at[kind, tick, seen],
                    place(delta),
                    pipe,
                )
            )
        if tick:
            push(
                remote(
                    source,
                    landing,
                    next_send(kind, tick),
                    w_recv.at[kind, tick, 0],
                    me,
                    pipe,
                )
            )

    def take_weight(kind, tick, phase):
        dims = grid.share_dims
        if phase == 0 and tick:
            landing = wholes[kind].at[tick, share_slot(grid.zero)]
            remote(
                landing,
                landing,
                w_send.at[kind, tick, 0],
                w_recv.at[kind, tick, 0],
                me,
                (section + pipe_count - tick) % pipe_count,
            ).wait_recv()
        for delta in grid.share:
            if delta[dims[phase]] == 0 or any(delta[d] for d in dims[phase + 1 :]):
                continue
            landing = wholes[kind].at[tick, share_slot(delta)]
            remote(
                landing,
                landing,
                w_send.at[kind, tick, 0],
                w_recv.at[kind, tick, grid.share.index(delta)],
                place(grid.along(dims[phase], 1)),
            ).wait_recv()
            for dim in dims[phase + 1 :]:
                for by in range(1, sizes[dim]):
                    hop = grid.along(dim, by)
                    seen = grid.share.index(grid.minus(delta, hop))
                    push(
                        remote(
                            landing,
                            landing,
                            next_send(kind, tick),
                            w_recv.at[kind, tick, seen],
                            place(hop),
                        )
                    )

    phases = range(len(grid.share_dims))
    layered = [kept, next_kept]

    def project(kind, tick, h):
        part = [part_keyval, part_query][kind]
        came = [came_keyval, came_query][kind]
        send, recv = [(pk_send, pk_recv), (pq_send, pq_recv)][kind]
        width = part.shape[-1]
        value = layered[tick][h].reshape(stacked, wide)
        weight = wholes[kind][tick].reshape(wide, width)
        total = jnp.dot(value, weight, preferred_element_type=FULL).astype(LOW)
        part[tick, h] = total.reshape(split_count, half, width)
        for index, delta in enumerate(grid.split):
            if delta != grid.zero:
                seen = grid.split.index(grid.minus(grid.zero, delta))
                push(
                    remote(
                        part.at[tick, h, split_slot(delta)],
                        came.at[tick, h, seen],
                        send.at[tick, h, index],
                        recv.at[tick, h, seen],
                        place(delta),
                    )
                )

    def summed(kind, tick, h):
        part = [part_keyval, part_query][kind]
        came = [came_keyval, came_query][kind]
        send, recv = [(pk_send, pk_recv), (pq_send, pq_recv)][kind]
        total = part[tick, h, split_slot(grid.zero)].astype(FULL)
        for index, delta in enumerate(grid.split):
            if delta != grid.zero:
                landing = came.at[tick, h, index]
                remote(
                    landing,
                    landing,
                    send.at[tick, h, index],
                    recv.at[tick, h, index],
                    place(delta),
                ).wait_recv()
                total += came[tick, h, index].astype(FULL)
        return (total * factors[tick, h]).astype(LOW)

    def send_squares(h, total):
        ones = jnp.ones((8, 128), FULL)
        for index, delta in enumerate(grid.split):
            piece = total[index * half : (index + 1) * half]
            piece = jnp.concatenate([piece] * (128 // half), axis=0)
            part_square[h, index] = lax.dot_general(
                ones,
                piece,
                (((1,), (1,)), ((), ())),
                preferred_element_type=FULL,
                precision=lax.Precision.HIGHEST,
            )
        for index, delta in enumerate(grid.split):
            if delta != grid.zero:
                seen = grid.split.index(grid.minus(grid.zero, delta))
                push(
                    remote(
                        part_square.at[h, split_slot(delta)],
                        came_square.at[h, seen],
                        sq_send.at[h, index],
                        sq_recv.at[h, seen],
                        place(delta),
                    )
                )

    def take_squares(h):
        total = part_square[h, split_slot(grid.zero)]
        for index, delta in enumerate(grid.split):
            if delta != grid.zero:
                landing = came_square.at[h, index]
                remote(
                    landing, landing, sq_send.at[h, index], sq_recv.at[h, index], place(delta)
                ).wait_recv()
                total += came_square[h, index]
        column = jnp.transpose(total)[:half, 0:1]
        factors[1, h] = lax.rsqrt(column / model_width + 1e-05)

    def before(h, delta):
        theirs = grid.within(moved(delta), grid.major_dims)
        ours = grid.within(coords, grid.major_dims)
        return theirs < ours if h == 0 else theirs > ours

    def after(h, delta):
        theirs = grid.within(moved(delta), grid.major_dims)
        ours = grid.within(coords, grid.major_dims)
        return theirs > ours if h == 0 else theirs < ours

    def relay(tick, h, delta, hop, when):
        landing = keyvals.at[tick, h, rank_of(h, delta)]
        seen = grid.minus(delta, hop)
        push(
            remote(
                landing,
                landing,
                kv_send.at[tick, h, grid.flat(grid.plus(delta, hop))],
                kv_recv.at[tick, h, grid.flat(seen)],
                place(hop),
            ),
            when,
        )

    def send_keyvals(tick, h):
        keyvals[tick, h, rank_of(h, grid.zero)] = summed(0, tick, h)
        for delta in grid.major:
            if delta != grid.zero:
                relay(tick, h, grid.zero, delta, after(h, delta))
        for hop in grid.minor:
            if hop != grid.zero:
                relay(tick, h, grid.zero, hop, None)

    def wait_keyvals(tick, h, delta):
        landing = keyvals.at[tick, h, rank_of(h, delta)]
        remote(
            landing,
            landing,
            kv_send.at[tick, h, 0],
            kv_recv.at[tick, h, grid.flat(delta)],
            place(grid.along(0, 1)),
        ).wait_recv()

    def pass_keyvals(tick, h):
        for delta in grid.major:
            if delta != grid.zero:
                when = before(h, delta)
                pl.when(when)(functools.partial(wait_keyvals, tick, h, delta))
                for hop in grid.minor:
                    if hop != grid.zero:
                        relay(tick, h, delta, hop, when)

    def take_keyvals(tick, h):
        for hop in grid.minor:
            if hop != grid.zero:
                wait_keyvals(tick, h, hop)
        for delta in grid.major:
            if delta != grid.zero:

                @pl.when(before(h, delta))
                def _(delta=delta):
                    for hop in grid.minor:
                        if hop != grid.zero:
                            wait_keyvals(tick, h, grid.plus(delta, hop))

    def attend(tick, h):
        query = summed(1, tick, h)
        query = jnp.concatenate(
            [query[:, i * head_dim : (i + 1) * head_dim] for i in range(head_count)], axis=0
        )
        take_keyvals(tick, h)
        keys = keyvals[tick, h, :, :, :head_dim].reshape(ctx_count * half, head_dim)
        values = keyvals[tick, h, :, :, head_dim:].reshape(ctx_count * half, head_dim)
        scores = lax.dot_general(
            query, keys, (((1,), (1,)), ((), ())), preferred_element_type=FULL
        )
        scores = scores.reshape(head_count, half, ctx_count * half) * scale + bias[h][None]
        probs = jnp.exp(scores - jnp.max(scores, axis=-1, keepdims=True))
        totals = jnp.sum(probs, axis=-1, keepdims=True)
        mixed = jnp.dot(
            probs.astype(LOW).reshape(head_count * half, ctx_count * half),
            values,
            preferred_element_type=FULL,
        ).reshape(head_count, half, head_dim)
        mixed = (mixed / totals).astype(LOW)
        own = attended.at[tick, h, split_slot(grid.zero)]
        for i in range(head_count):
            own[:, i * head_dim : (i + 1) * head_dim] = mixed[i]
        for index, delta in enumerate(grid.split):
            if delta != grid.zero:
                seen = grid.split.index(grid.minus(grid.zero, delta))
                push(
                    remote(
                        own,
                        own,
                        at_send.at[tick, h, index],
                        at_recv.at[tick, h, seen],
                        place(delta),
                    )
                )

    def take_attended(tick, h):
        for index, delta in enumerate(grid.split):
            if delta != grid.zero:
                landing = attended.at[tick, h, split_slot(delta)]
                remote(
                    landing,
                    landing,
                    at_send.at[tick, h, index],
                    at_recv.at[tick, h, index],
                    place(delta),
                ).wait_recv()

    def mix_first(h):
        take_attended(0, h)
        value = attended[0, h].reshape(stacked, query_width)
        squares = jnp.zeros((stacked, 128), FULL)
        for s in range(share_count):
            cols = pl.ds(s * block, block)
            mixed = jnp.dot(value, w_out[0, s], preferred_element_type=FULL)
            first_sum[h, :, :, cols] = mixed.reshape(split_count, half, block)
            following = kept[h, :, :, cols].reshape(stacked, block).astype(FULL) + mixed
            next_kept[h, :, :, cols] = following.astype(LOW).reshape(split_count, half, block)
            following = following * following
            for c in range(0, block, 128):
                squares += following[:, c : c + 128]
        send_squares(h, squares)

    def mix_last(h):
        take_attended(1, h)
        value = attended[1, h].reshape(stacked, query_width)
        for s in range(share_count):
            cols = pl.ds(s * block, block)
            mixed = jnp.dot(value, w_out[1, s], preferred_element_type=FULL)
            mixed = mixed.reshape(split_count, half, block) + first_sum[h, :, :, cols]
            back[h, :, :, cols] = mixed.astype(LOW)
        for index, delta in enumerate(grid.split):
            if delta != grid.zero:
                seen = grid.split.index(grid.minus(grid.zero, delta))
                push(
                    remote(
                        back.at[h, split_slot(delta)],
                        came_back.at[h, seen],
                        b_send.at[h, index],
                        b_recv.at[h, seen],
                        place(delta),
                    )
                )

    def end(h):
        for index, delta in enumerate(grid.split):
            if delta == grid.zero:
                source = back.at[h, split_slot(grid.zero)]
            else:
                source = came_back.at[h, index]
                remote(
                    source, source, b_send.at[h, index], b_recv.at[h, index], place(delta)
                ).wait_recv()
            for share in grid.share:
                cols = columns(place(grid.plus(delta, share)))
                value = source[:, columns(share_slot(share))].astype(FULL)
                result[rows(h), cols] = stream[rows(h), cols] + value

    halves = range(HALVES)
    send_stream(0)
    load_gain.wait()
    load_keyval.wait()
    fill(0, 0)
    begin(0, 0)
    send_stream(1)
    load_query.wait()
    load_out.wait()
    fill(1, 0)
    fill(2, 0)
    for kind in range(3):
        fill(kind, 1)
    for phase in phases:
        take_weight(0, 0, phase)
    take_stream(0)
    begin(1, 0)
    project(0, 0, 0)
    take_stream(1)
    project(0, 0, 1)
    for h in halves:
        send_keyvals(0, h)
    take_weight(1, 0, 0)
    begin(2, 0)
    for h in halves:
        pass_keyvals(0, h)
    for phase in phases[1:]:
        take_weight(1, 0, phase)
    for h in halves:
        project(1, 0, h)
    begin(0, 1)
    take_weight(2, 0, 0)
    begin(1, 1)
    for h in halves:
        attend(0, h)
    for phase in phases[1:]:
        take_weight(2, 0, phase)
    take_weight(0, 1, 0)
    mix_first(0)
    for phase in phases[1:]:
        take_weight(0, 1, phase)
    project(0, 1, 0)
    mix_first(1)
    project(0, 1, 1)
    for h in halves:
        take_squares(h)
        send_keyvals(1, h)
    take_weight(1, 1, 0)
    begin(2, 1)
    for h in halves:
        pass_keyvals(1, h)
    for phase in phases[1:]:
        take_weight(1, 1, phase)
    for h in halves:
        project(1, 1, h)
    take_weight(2, 1, 0)
    for h in halves:
        attend(1, h)
    for phase in phases[1:]:
        take_weight(2, 1, phase)
    for h in halves:
        mix_last(h)
    for h in halves:
        end(h)
    for copy, when in finish:
        if when is None:
            copy.wait_send()
        else:
            pl.when(when)(copy.wait_send)


def run_layers(order, stream, gain, query, keyval, out, segments, ctx_count):
    grid = Grid(ctx_count)
    split, share = len(grid.split), len(grid.share)
    tok_rows, model_width = stream.shape
    half = tok_rows // HALVES
    block = model_width // ctx_count
    wide = block * share
    query_width, kv_width = query.shape[-1], keyval.shape[-1]
    vmem = pl.BlockSpec(memory_space=pltpu.VMEM)
    hbm = pl.BlockSpec(memory_space=pl.ANY)
    smem = pl.BlockSpec(memory_space=pltpu.SMEM)
    dma = pltpu.SemaphoreType.DMA
    scratch = [
        pltpu.VMEM(stream.shape, FULL),
        pltpu.VMEM(gain.shape, LOW),
        pltpu.VMEM(query.shape, LOW),
        pltpu.VMEM(keyval.shape, LOW),
        pltpu.VMEM(out.shape, LOW),
        pltpu.VMEM((HALVES, split, half, wide), LOW),
        pltpu.VMEM((HALVES, split, half, wide), LOW),
        pltpu.VMEM((HALVES, split, half, wide), LOW),
        pltpu.VMEM((HALVES, split, half, wide), FULL),
        pltpu.VMEM((TICKS, share, block, kv_width), LOW),
        pltpu.VMEM((TICKS, share, block, query_width), LOW),
        pltpu.VMEM((TICKS, share, query_width, block), LOW),
        pltpu.VMEM((block, kv_width), LOW),
        pltpu.VMEM((block, query_width), LOW),
        pltpu.VMEM((query_width, block), LOW),
        pltpu.VMEM((TICKS, HALVES, split, half, kv_width), LOW),
        pltpu.VMEM((TICKS, HALVES, split, half, query_width), LOW),
        pltpu.VMEM((TICKS, HALVES, split, half, kv_width), LOW),
        pltpu.VMEM((TICKS, HALVES, split, half, query_width), LOW),
        pltpu.VMEM((HALVES, split, 8, 128), FULL),
        pltpu.VMEM((HALVES, split, 8, 128), FULL),
        pltpu.VMEM((TICKS, HALVES, ctx_count, half, kv_width), LOW),
        pltpu.VMEM((TICKS, HALVES, split, half, query_width), LOW),
        pltpu.VMEM((HALVES, split, half, wide), LOW),
        pltpu.VMEM((HALVES, split, half, wide), LOW),
        pltpu.VMEM((HALVES, half, ctx_count * half), FULL),
        dma((8,)),
        dma((HALVES, split)),
        dma((HALVES, split)),
        dma((3, TICKS, share + 2)),
        dma((3, TICKS, share)),
    ]
    scratch += [dma((TICKS, HALVES, split))] * 4
    scratch += [dma((HALVES, split))] * 2
    scratch += [dma((TICKS, HALVES, ctx_count))] * 2
    scratch += [dma((TICKS, HALVES, split))] * 2
    scratch += [dma((HALVES, split))] * 2
    return pl.pallas_call(
        functools.partial(layers_kernel, grid),
        out_shape=jax.ShapeDtypeStruct(stream.shape, FULL),
        in_specs=[smem] + [hbm] * 5 + [vmem],
        out_specs=vmem,
        scratch_shapes=scratch,
        compiler_params=pltpu.CompilerParams(
            collective_id=0, has_side_effects=True, vmem_limit_bytes=56 * 1024 * 1024
        ),
    )(order, stream, gain, query, keyval, out, segments)


def body(activations, norm_gain, w_query, w_keyval, w_out, segment_ids, layer_order):
    ctx_count = lax.axis_size("ctx")
    pipe_count = lax.axis_size("pipe")
    state = run_layers(
        layer_order.reshape(1, TICKS),
        activations[0, 0],
        norm_gain[0],
        w_query[0],
        w_keyval[0],
        w_out[0],
        segment_ids,
        ctx_count,
    )
    if TICKS % pipe_count:
        pairs = [(i, (i + TICKS) % pipe_count) for i in range(pipe_count)]
        state = lax.ppermute(state, "pipe", pairs)
    return state[None, None]


def solution(mesh):
    in_specs = (
        P("pipe", None, "ctx", None),
        P("pipe", None, "ctx"),
        P("pipe", None, "ctx", None),
        P("pipe", None, "ctx", None),
        P("pipe", None, None, "ctx"),
        P(),
        P(None, "pipe"),
    )
    out_specs = P("pipe", None, "ctx", None)
    return jax.shard_map(body, mesh=mesh, in_specs=in_specs, out_specs=out_specs, check_vma=False)
```

```python
import functools
import itertools
import math

import jax
import jax.numpy as jnp
from jax import lax
from jax.experimental import pallas as pl
from jax.experimental.pallas import tpu as pltpu
from jax.sharding import PartitionSpec as P

TICKS = 2
HALVES = 2
MESH = pl.DeviceIdType.MESH
LOW = jnp.bfloat16
FULL = jnp.float32


def grid_of(count):
    known = {
        16: ((2, 2, 2, 2), (1, 3), (0, 2), (0, 1), (2, 3)),
        32: ((4, 8), (0,), (1,), (0,), (1,)),
    }
    return known[count]


class Grid:
    def __init__(self, count):
        self.sizes, self.split_dims, self.share_dims, self.major_dims, self.minor_dims = grid_of(count)
        self.rank = len(self.sizes)
        self.strides = [math.prod(self.sizes[d + 1 :]) for d in range(self.rank)]
        self.split = self.deltas(self.split_dims)
        self.share = self.deltas(self.share_dims)
        self.major = self.deltas(self.major_dims)
        self.minor = self.deltas(self.minor_dims)
        self.hops = [
            self.along(d, by) for d in self.share_dims for by in range(1, self.sizes[d])
        ]
        self.zero = (0,) * self.rank
        self.relayed = self.sizes[:2] == (2, 2)

    def deltas(self, dims):
        ranges = [range(self.sizes[d]) if d in dims else range(1) for d in range(self.rank)]
        return list(itertools.product(*ranges))

    def along(self, dim, by):
        return tuple(by if d == dim else 0 for d in range(self.rank))

    def flat(self, delta):
        return sum(delta[d] * self.strides[d] for d in range(self.rank))

    def minus(self, one, other):
        return tuple((a - b) % s for a, b, s in zip(one, other, self.sizes))

    def plus(self, one, other):
        return tuple((a + b) % s for a, b, s in zip(one, other, self.sizes))

    def within(self, coords, dims):
        total = 0
        for d in dims:
            total = total * self.sizes[d] + coords[d]
        return total


def layers_kernel(grid, *refs):
    order, stream_hbm, gain_hbm, query_hbm, keyval_hbm, out_hbm, segments = refs[:7]
    result = refs[7]
    (
        stream,
        gains,
        query_all,
        keyval_all,
        out_all,
        sent,
        kept,
        next_kept,
        first_sum,
        w_keyval,
        w_query,
        w_out,
        later_keyval,
        later_query,
        later_out,
        relay_keyval,
        relay_query,
        relay_out,
        part_keyval,
        part_query,
        came_keyval,
        came_query,
        part_square,
        came_square,
        keyvals,
        attended,
        back,
        came_back,
        bias,
        load_sems,
        x_send,
        x_recv,
        w_send,
        w_recv,
        r_send,
        r_recv,
        pk_send,
        pk_recv,
        pq_send,
        pq_recv,
        sq_send,
        sq_recv,
        kv_send,
        kv_recv,
        at_send,
        at_recv,
        b_send,
        b_recv,
    ) = refs[8:]
    sizes = grid.sizes
    ctx_count = math.prod(sizes)
    me = lax.axis_index("ctx")
    section = lax.axis_index("pipe")
    pipe_count = lax.axis_size("pipe")
    coords = [(me // grid.strides[d]) % sizes[d] for d in range(grid.rank)]
    split_count, share_count = len(grid.split), len(grid.share)
    tok_rows, model_width = stream.shape
    half = tok_rows // HALVES
    block = model_width // ctx_count
    wide = block * share_count
    query_width = w_query.shape[-1]
    kv_width = w_keyval.shape[-1]
    head_dim = kv_width // 2
    head_count = query_width // head_dim
    scale = 1.0 / math.sqrt(head_dim)
    stacked = split_count * half

    def moved(delta):
        return [(coords[d] + delta[d]) % sizes[d] for d in range(grid.rank)]

    def place(delta):
        return sum(c * s for c, s in zip(moved(delta), grid.strides))

    def split_slot(delta):
        return grid.within(moved(delta), grid.split_dims)

    def share_slot(delta):
        return grid.within(moved(delta), grid.share_dims)

    def rank_of(half_index, delta):
        where = place(delta)
        return where if half_index == 0 else ctx_count - 1 - where

    def columns(index):
        return pl.ds(pl.multiple_of(index * block, block), block)

    def rows(half_index):
        return pl.ds(half_index * half, half)

    finish = []

    def remote(src, dst, send, recv, ctx, pipe=None):
        device = {"ctx": ctx} if pipe is None else {"ctx": ctx, "pipe": pipe}
        return pltpu.make_async_remote_copy(
            src_ref=src,
            dst_ref=dst,
            send_sem=send,
            recv_sem=recv,
            device_id=device,
            device_id_type=MESH,
        )

    def push(copy, when=None):
        if when is None:
            copy.start()
        else:
            pl.when(when)(copy.start)
        finish.append((copy, when))

    loads = []

    def load(src, dst):
        copy = pltpu.make_async_copy(src, dst, load_sems.at[len(loads)])
        copy.start()
        loads.append(copy)
        return copy

    load_stream = [load(stream_hbm.at[rows(h)], stream.at[rows(h)]) for h in range(HALVES)]
    load_gain = load(gain_hbm, gains)
    load_keyval = load(keyval_hbm, keyval_all)
    load_query = load(query_hbm, query_all)
    load_out = load(out_hbm, out_all)

    keyvals[...] = jnp.zeros_like(keyvals)

    near = sorted(
        set(grid.split + grid.hops + grid.major + grid.minor) - {grid.zero}
    )
    barrier = pltpu.get_barrier_semaphore()
    greeted = 0
    for delta in near:
        pl.semaphore_signal(
            barrier, inc=1, device_id={"ctx": place(delta)}, device_id_type=MESH
        )
        greeted += 1
    for by in sorted({1, pipe_count - 1}):
        for delta in sorted(set([grid.zero] + grid.hops + grid.major)):
            pl.semaphore_signal(
                barrier,
                inc=1,
                device_id={"ctx": place(delta), "pipe": (section + by) % pipe_count},
                device_id_type=MESH,
            )
            greeted += 1

    key_rel = lax.broadcasted_iota(jnp.int32, (half, ctx_count * half), 1)
    row_rel = lax.broadcasted_iota(jnp.int32, (half, ctx_count * half), 0)
    for h in range(HALVES):
        query_rel = row_rel + rank_of(h, grid.zero) * half
        seg = segments[:, h * ctx_count * half : (h + 1) * ctx_count * half].astype(FULL)
        seg = jnp.broadcast_to(seg, (half, ctx_count * half))
        own = jnp.sum(jnp.where(key_rel == query_rel, seg, 0.0), axis=1, keepdims=True)
        bias[h] = jnp.where((key_rel <= query_rel) & (seg == own), 0.0, -1e30)

    pl.semaphore_wait(barrier, greeted)

    others = [delta for delta in grid.split if delta != grid.zero]
    factors = {}

    def send_stream(h):
        load_stream[h].wait()
        squares = jnp.zeros((half, 1), FULL)
        for index, delta in enumerate(grid.split):
            target = kept.at[h, split_slot(grid.zero)] if delta == grid.zero else sent.at[h, index]
            for s, share in enumerate(grid.share):
                where = grid.plus(delta, share)
                value = stream[rows(h), columns(place(where))]
                squares += jnp.sum(value * value, axis=1, keepdims=True)
                target[:, columns(share_slot(share))] = value.astype(LOW)
            if delta != grid.zero:
                seen = grid.split.index(grid.minus(grid.zero, delta))
                push(
                    remote(
                        sent.at[h, index],
                        kept.at[h, split_slot(grid.zero)],
                        x_send.at[h, index],
                        x_recv.at[h, seen],
                        place(delta),
                    )
                )
        factors[0, h] = lax.rsqrt(squares / model_width + 1e-05)

    def take_stream(h):
        for index, delta in enumerate(grid.split):
            if delta != grid.zero:
                landing = kept.at[h, split_slot(delta)]
                remote(
                    landing, landing, x_send.at[h, index], x_recv.at[h, index], place(delta)
                ).wait_recv()

    wholes = [w_keyval, w_query, w_out]
    laters = [later_keyval, later_query, later_out]
    used = {}

    def fill(kind, tick):
        layer = order[0, tick]
        source = [keyval_all, query_all, out_all][kind]
        value = source[layer]
        if kind < 2:
            level = lax.broadcasted_iota(jnp.int32, gains.shape, 0)
            gain = jnp.where(level == layer, gains[...].astype(FULL), 0.0)
            gain = jnp.sum(gain, axis=0, keepdims=True)
            gain = jnp.transpose(jnp.broadcast_to(gain, (128, block)))
            value = value.astype(FULL)
            value = jnp.concatenate(
                [value[:, c : c + 128] * gain for c in range(0, value.shape[1], 128)], axis=1
            ).astype(LOW)
        if tick == 0:
            wholes[kind][tick, share_slot(grid.zero)] = value
        else:
            laters[kind][...] = value

    def next_send(kind, tick):
        count = used.get((kind, tick), 0)
        used[kind, tick] = count + 1
        return w_send.at[kind, tick, count]

    line = coords[0] * 2 + coords[1] if grid.relayed else 0
    middle = (line + 1) // 2 == 1 if grid.relayed else False
    relays = [relay_keyval, relay_query, relay_out]

    def on_line(where):
        return me + (where - line) * grid.strides[1]

    def begin(kind, tick):
        slot = share_slot(grid.zero)
        landing = wholes[kind].at[tick, slot]
        source = landing if tick == 0 else laters[kind]
        pipe = None if tick == 0 else (section + pipe_count - tick) % pipe_count
        for delta in grid.hops + [grid.zero] * (tick > 0):
            seen = grid.share.index(grid.minus(grid.zero, delta))
            recv = w_recv.at[kind, tick, seen]
            target, where = landing, place(delta)
            if grid.relayed and delta[0]:
                recv = r_recv.at[kind, tick, coords[0]]
                target, where = relays[kind].at[tick, coords[0]], on_line(1 + line % 2)
            push(remote(source, target, next_send(kind, tick), recv, where, pipe))

    def relay_weight(kind, tick):
        if not grid.relayed:
            return
        for origin in range(2):
            landing = relays[kind].at[tick, origin]
            arrival = remote(
                landing,
                landing,
                r_send.at[kind, tick, origin],
                r_recv.at[kind, tick, origin],
                on_line(line - 1 + 2 * (1 - origin)),
            )
            pl.when(middle)(arrival.wait_recv)
            seen = grid.share.index(grid.along(0, 1))
            slot = origin * sizes[2] + coords[2]
            push(
                remote(
                    landing,
                    wholes[kind].at[tick, slot],
                    r_send.at[kind, tick, origin],
                    w_recv.at[kind, tick, seen],
                    on_line(line - 1 + 2 * (1 - origin)),
                ),
                middle,
            )

    def take_weight(kind, tick, phase):
        dims = grid.share_dims
        if phase == 0 and tick:
            landing = wholes[kind].at[tick, share_slot(grid.zero)]
            remote(
                landing,
                landing,
                w_send.at[kind, tick, 0],
                w_recv.at[kind, tick, 0],
                me,
                (section + pipe_count - tick) % pipe_count,
            ).wait_recv()
        for delta in grid.share:
            if delta[dims[phase]] == 0 or any(delta[d] for d in dims[phase + 1 :]):
                continue
            landing = wholes[kind].at[tick, share_slot(delta)]
            remote(
                landing,
                landing,
                w_send.at[kind, tick, 0],
                w_recv.at[kind, tick, grid.share.index(delta)],
                place(grid.along(dims[phase], 1)),
            ).wait_recv()
            for dim in dims[phase + 1 :]:
                for by in range(1, sizes[dim]):
                    hop = grid.along(dim, by)
                    seen = grid.share.index(grid.minus(delta, hop))
                    push(
                        remote(
                            landing,
                            landing,
                            next_send(kind, tick),
                            w_recv.at[kind, tick, seen],
                            place(hop),
                        )
                    )

    phases = range(len(grid.share_dims))
    layered = [kept, next_kept]

    def project(kind, tick, h):
        part = [part_keyval, part_query][kind]
        came = [came_keyval, came_query][kind]
        send, recv = [(pk_send, pk_recv), (pq_send, pq_recv)][kind]
        width = part.shape[-1]
        value = layered[tick][h].reshape(stacked, wide)
        weight = wholes[kind][tick].reshape(wide, width)
        total = jnp.dot(value, weight, preferred_element_type=FULL).astype(LOW)
        part[tick, h] = total.reshape(split_count, half, width)
        for index, delta in enumerate(grid.split):
            if delta != grid.zero:
                seen = grid.split.index(grid.minus(grid.zero, delta))
                push(
                    remote(
                        part.at[tick, h, split_slot(delta)],
                        came.at[tick, h, seen],
                        send.at[tick, h, index],
                        recv.at[tick, h, seen],
                        place(delta),
                    )
                )

    def summed(kind, tick, h):
        part = [part_keyval, part_query][kind]
        came = [came_keyval, came_query][kind]
        send, recv = [(pk_send, pk_recv), (pq_send, pq_recv)][kind]
        total = part[tick, h, split_slot(grid.zero)].astype(FULL)
        for index, delta in enumerate(grid.split):
            if delta != grid.zero:
                landing = came.at[tick, h, index]
                remote(
                    landing,
                    landing,
                    send.at[tick, h, index],
                    recv.at[tick, h, index],
                    place(delta),
                ).wait_recv()
                total += came[tick, h, index].astype(FULL)
        return (total * factors[tick, h]).astype(LOW)

    def send_squares(h, total):
        ones = jnp.ones((8, 128), FULL)
        for index, delta in enumerate(grid.split):
            piece = total[index * half : (index + 1) * half]
            piece = jnp.concatenate([piece] * (128 // half), axis=0)
            part_square[h, index] = lax.dot_general(
                ones,
                piece,
                (((1,), (1,)), ((), ())),
                preferred_element_type=FULL,
                precision=lax.Precision.HIGHEST,
            )
        for index, delta in enumerate(grid.split):
            if delta != grid.zero:
                seen = grid.split.index(grid.minus(grid.zero, delta))
                push(
                    remote(
                        part_square.at[h, split_slot(delta)],
                        came_square.at[h, seen],
                        sq_send.at[h, index],
                        sq_recv.at[h, seen],
                        place(delta),
                    )
                )

    def take_squares(h):
        total = part_square[h, split_slot(grid.zero)]
        for index, delta in enumerate(grid.split):
            if delta != grid.zero:
                landing = came_square.at[h, index]
                remote(
                    landing, landing, sq_send.at[h, index], sq_recv.at[h, index], place(delta)
                ).wait_recv()
                total += came_square[h, index]
        column = jnp.transpose(total)[:half, 0:1]
        factors[1, h] = lax.rsqrt(column / model_width + 1e-05)

    def before(h, delta):
        theirs = grid.within(moved(delta), grid.major_dims)
        ours = grid.within(coords, grid.major_dims)
        return theirs < ours if h == 0 else theirs > ours

    def after(h, delta):
        theirs = grid.within(moved(delta), grid.major_dims)
        ours = grid.within(coords, grid.major_dims)
        return theirs > ours if h == 0 else theirs < ours

    def relay(tick, h, delta, hop, when):
        landing = keyvals.at[tick, h, rank_of(h, delta)]
        seen = grid.minus(delta, hop)
        push(
            remote(
                landing,
                landing,
                kv_send.at[tick, h, grid.flat(grid.plus(delta, hop))],
                kv_recv.at[tick, h, grid.flat(seen)],
                place(hop),
            ),
            when,
        )

    def send_keyvals(tick, h):
        keyvals[tick, h, rank_of(h, grid.zero)] = summed(0, tick, h)
        for delta in grid.major:
            if delta != grid.zero:
                relay(tick, h, grid.zero, delta, after(h, delta))
        for hop in grid.minor:
            if hop != grid.zero:
                relay(tick, h, grid.zero, hop, rank_of(h, hop) > rank_of(h, grid.zero))

    def wait_keyvals(tick, h, delta):
        landing = keyvals.at[tick, h, rank_of(h, delta)]
        remote(
            landing,
            landing,
            kv_send.at[tick, h, 0],
            kv_recv.at[tick, h, grid.flat(delta)],
            place(grid.along(0, 1)),
        ).wait_recv()

    def pass_keyvals(tick, h):
        for delta in grid.major:
            if delta != grid.zero:
                when = before(h, delta)
                pl.when(when)(functools.partial(wait_keyvals, tick, h, delta))
                for hop in grid.minor:
                    if hop != grid.zero:
                        relay(tick, h, delta, hop, when)

    def take_keyvals(tick, h):
        for hop in grid.minor:
            if hop != grid.zero:
                when = rank_of(h, hop) < rank_of(h, grid.zero)
                pl.when(when)(functools.partial(wait_keyvals, tick, h, hop))
        for delta in grid.major:
            if delta != grid.zero:

                @pl.when(before(h, delta))
                def _(delta=delta):
                    for hop in grid.minor:
                        if hop != grid.zero:
                            wait_keyvals(tick, h, grid.plus(delta, hop))

    def attend(tick, h):
        query = summed(1, tick, h)
        query = jnp.concatenate(
            [query[:, i * head_dim : (i + 1) * head_dim] for i in range(head_count)], axis=0
        )
        take_keyvals(tick, h)
        keys = keyvals[tick, h, :, :, :head_dim].reshape(ctx_count * half, head_dim)
        values = keyvals[tick, h, :, :, head_dim:].reshape(ctx_count * half, head_dim)
        scores = lax.dot_general(
            query, keys, (((1,), (1,)), ((), ())), preferred_element_type=FULL
        )
        scores = scores.reshape(head_count, half, ctx_count * half) * scale + bias[h][None]
        probs = jnp.exp(scores - jnp.max(scores, axis=-1, keepdims=True))
        totals = jnp.sum(probs, axis=-1, keepdims=True)
        mixed = jnp.dot(
            probs.astype(LOW).reshape(head_count * half, ctx_count * half),
            values,
            preferred_element_type=FULL,
        ).reshape(head_count, half, head_dim)
        mixed = (mixed / totals).astype(LOW)
        own = attended.at[tick, h, split_slot(grid.zero)]
        for i in range(head_count):
            own[:, i * head_dim : (i + 1) * head_dim] = mixed[i]
        for index, delta in enumerate(grid.split):
            if delta != grid.zero:
                seen = grid.split.index(grid.minus(grid.zero, delta))
                push(
                    remote(
                        own,
                        own,
                        at_send.at[tick, h, index],
                        at_recv.at[tick, h, seen],
                        place(delta),
                    )
                )

    def take_attended(tick, h):
        for index, delta in enumerate(grid.split):
            if delta != grid.zero:
                landing = attended.at[tick, h, split_slot(delta)]
                remote(
                    landing,
                    landing,
                    at_send.at[tick, h, index],
                    at_recv.at[tick, h, index],
                    place(delta),
                ).wait_recv()

    def mix_first(h):
        take_attended(0, h)
        value = attended[0, h].reshape(stacked, query_width)
        squares = jnp.zeros((stacked, 128), FULL)
        for s in range(share_count):
            cols = pl.ds(s * block, block)
            mixed = jnp.dot(value, w_out[0, s], preferred_element_type=FULL)
            first_sum[h, :, :, cols] = mixed.reshape(split_count, half, block)
            following = kept[h, :, :, cols].reshape(stacked, block).astype(FULL) + mixed
            next_kept[h, :, :, cols] = following.astype(LOW).reshape(split_count, half, block)
            following = following * following
            for c in range(0, block, 128):
                squares += following[:, c : c + 128]
        send_squares(h, squares)

    def mix_last(h):
        take_attended(1, h)
        value = attended[1, h].reshape(stacked, query_width)
        for s in range(share_count):
            cols = pl.ds(s * block, block)
            mixed = jnp.dot(value, w_out[1, s], preferred_element_type=FULL)
            mixed = mixed.reshape(split_count, half, block) + first_sum[h, :, :, cols]
            back[h, :, :, cols] = mixed.astype(LOW)
        for index, delta in enumerate(grid.split):
            if delta != grid.zero:
                seen = grid.split.index(grid.minus(grid.zero, delta))
                push(
                    remote(
                        back.at[h, split_slot(delta)],
                        came_back.at[h, seen],
                        b_send.at[h, index],
                        b_recv.at[h, seen],
                        place(delta),
                    )
                )

    def end(h):
        for index, delta in enumerate(grid.split):
            if delta == grid.zero:
                source = back.at[h, split_slot(grid.zero)]
            else:
                source = came_back.at[h, index]
                remote(
                    source, source, b_send.at[h, index], b_recv.at[h, index], place(delta)
                ).wait_recv()
            for share in grid.share:
                cols = columns(place(grid.plus(delta, share)))
                result[rows(h), cols] = source[:, columns(share_slot(share))]

    halves = range(HALVES)
    send_stream(0)
    load_gain.wait()
    load_keyval.wait()
    fill(0, 0)
    begin(0, 0)
    send_stream(1)
    load_query.wait()
    load_out.wait()
    fill(1, 0)
    begin(1, 0)
    fill(2, 0)
    relay_weight(0, 0)
    for kind in range(3):
        fill(kind, 1)
    for phase in phases:
        take_weight(0, 0, phase)
    take_stream(0)
    project(0, 0, 0)
    take_stream(1)
    project(0, 0, 1)
    begin(2, 0)
    relay_weight(1, 0)
    for h in halves:
        send_keyvals(0, h)
    take_weight(1, 0, 0)
    for h in halves:
        pass_keyvals(0, h)
    begin(0, 1)
    relay_weight(2, 0)
    for phase in phases[1:]:
        take_weight(1, 0, phase)
    for h in halves:
        project(1, 0, h)
    begin(1, 1)
    relay_weight(0, 1)
    take_weight(2, 0, 0)
    attend(0, 0)
    attend(0, 1)
    relay_weight(1, 1)
    take_weight(0, 1, 0)
    for phase in phases[1:]:
        take_weight(2, 0, phase)
    mix_first(0)
    for phase in phases[1:]:
        take_weight(0, 1, phase)
    project(0, 1, 0)
    mix_first(1)
    project(0, 1, 1)
    begin(2, 1)
    take_weight(1, 1, 0)
    for h in halves:
        take_squares(h)
        send_keyvals(1, h)
    relay_weight(2, 1)
    for h in halves:
        pass_keyvals(1, h)
    take_weight(2, 1, 0)
    for phase in phases[1:]:
        take_weight(1, 1, phase)
    for h in halves:
        project(1, 1, h)
    attend(1, 0)
    attend(1, 1)
    for phase in phases[1:]:
        take_weight(2, 1, phase)
    for h in halves:
        mix_last(h)
    for h in halves:
        end(h)
    for copy, when in finish:
        if when is None:
            copy.wait_send()
        else:
            pl.when(when)(copy.wait_send)


def run_layers(order, stream, gain, query, keyval, out, segments, ctx_count):
    grid = Grid(ctx_count)
    split, share = len(grid.split), len(grid.share)
    tok_rows, model_width = stream.shape
    half = tok_rows // HALVES
    block = model_width // ctx_count
    wide = block * share
    query_width, kv_width = query.shape[-1], keyval.shape[-1]
    vmem = pl.BlockSpec(memory_space=pltpu.VMEM)
    hbm = pl.BlockSpec(memory_space=pl.ANY)
    smem = pl.BlockSpec(memory_space=pltpu.SMEM)
    dma = pltpu.SemaphoreType.DMA
    scratch = [
        pltpu.VMEM(stream.shape, FULL),
        pltpu.VMEM(gain.shape, LOW),
        pltpu.VMEM(query.shape, LOW),
        pltpu.VMEM(keyval.shape, LOW),
        pltpu.VMEM(out.shape, LOW),
        pltpu.VMEM((HALVES, split, half, wide), LOW),
        pltpu.VMEM((HALVES, split, half, wide), LOW),
        pltpu.VMEM((HALVES, split, half, wide), LOW),
        pltpu.VMEM((HALVES, split, half, wide), FULL),
        pltpu.VMEM((TICKS, share, block, kv_width), LOW),
        pltpu.VMEM((TICKS, share, block, query_width), LOW),
        pltpu.VMEM((TICKS, share, query_width, block), LOW),
        pltpu.VMEM((block, kv_width), LOW),
        pltpu.VMEM((block, query_width), LOW),
        pltpu.VMEM((query_width, block), LOW),
        pltpu.VMEM((TICKS, 2, block, kv_width), LOW),
        pltpu.VMEM((TICKS, 2, block, query_width), LOW),
        pltpu.VMEM((TICKS, 2, query_width, block), LOW),
        pltpu.VMEM((TICKS, HALVES, split, half, kv_width), LOW),
        pltpu.VMEM((TICKS, HALVES, split, half, query_width), LOW),
        pltpu.VMEM((TICKS, HALVES, split, half, kv_width), LOW),
        pltpu.VMEM((TICKS, HALVES, split, half, query_width), LOW),
        pltpu.VMEM((HALVES, split, 8, 128), FULL),
        pltpu.VMEM((HALVES, split, 8, 128), FULL),
        pltpu.VMEM((TICKS, HALVES, ctx_count, half, kv_width), LOW),
        pltpu.VMEM((TICKS, HALVES, split, half, query_width), LOW),
        pltpu.VMEM((HALVES, split, half, wide), LOW),
        pltpu.VMEM((HALVES, split, half, wide), LOW),
        pltpu.VMEM((HALVES, half, ctx_count * half), FULL),
        dma((8,)),
        dma((HALVES, split)),
        dma((HALVES, split)),
        dma((3, TICKS, share + 2)),
        dma((3, TICKS, share)),
        dma((3, TICKS, 2)),
        dma((3, TICKS, 2)),
    ]
    scratch += [dma((TICKS, HALVES, split))] * 4
    scratch += [dma((HALVES, split))] * 2
    scratch += [dma((TICKS, HALVES, ctx_count))] * 2
    scratch += [dma((TICKS, HALVES, split))] * 2
    scratch += [dma((HALVES, split))] * 2
    return pl.pallas_call(
        functools.partial(layers_kernel, grid),
        out_shape=jax.ShapeDtypeStruct(stream.shape, LOW),
        in_specs=[smem] + [hbm] * 5 + [vmem],
        out_specs=vmem,
        scratch_shapes=scratch,
        compiler_params=pltpu.CompilerParams(
            collective_id=0, has_side_effects=True, vmem_limit_bytes=56 * 1024 * 1024
        ),
    )(order, stream, gain, query, keyval, out, segments)


def body(activations, norm_gain, w_query, w_keyval, w_out, segment_ids, layer_order):
    ctx_count = lax.axis_size("ctx")
    pipe_count = lax.axis_size("pipe")
    change = run_layers(
        layer_order.reshape(1, TICKS),
        activations[0, 0],
        norm_gain[0],
        w_query[0],
        w_keyval[0],
        w_out[0],
        segment_ids,
        ctx_count,
    )
    state = activations[0, 0] + change.astype(FULL)
    if TICKS % pipe_count:
        pairs = [(i, (i + TICKS) % pipe_count) for i in range(pipe_count)]
        state = lax.ppermute(state, "pipe", pairs)
    return state[None, None]


def solution(mesh):
    in_specs = (
        P("pipe", None, "ctx", None),
        P("pipe", None, "ctx"),
        P("pipe", None, "ctx", None),
        P("pipe", None, "ctx", None),
        P("pipe", None, None, "ctx"),
        P(),
        P(None, "pipe"),
    )
    out_specs = P("pipe", None, "ctx", None)
    return jax.shard_map(body, mesh=mesh, in_specs=in_specs, out_specs=out_specs, check_vma=False)
```

```python
import functools
import itertools
import math

import jax
import jax.numpy as jnp
from jax import lax
from jax.experimental import pallas as pl
from jax.experimental.pallas import tpu as pltpu
from jax.sharding import PartitionSpec as P

TICKS = 2
HALVES = 2
MESH = pl.DeviceIdType.MESH
LOW = jnp.bfloat16
FULL = jnp.float32


def grid_of(count):
    known = {
        16: ((2, 2, 2, 2), (1, 3), (0, 2), (0, 1), (2, 3)),
        32: ((4, 8), (0,), (1,), (0,), (1,)),
    }
    return known[count]


class Grid:
    def __init__(self, count):
        self.sizes, self.split_dims, self.share_dims, self.major_dims, self.minor_dims = grid_of(count)
        self.rank = len(self.sizes)
        self.strides = [math.prod(self.sizes[d + 1 :]) for d in range(self.rank)]
        self.split = self.deltas(self.split_dims)
        self.share = self.deltas(self.share_dims)
        self.major = self.deltas(self.major_dims)
        self.minor = self.deltas(self.minor_dims)
        self.hops = [
            self.along(d, by) for d in self.share_dims for by in range(1, self.sizes[d])
        ]
        self.zero = (0,) * self.rank
        self.relayed = self.sizes[:2] == (2, 2)

    def deltas(self, dims):
        ranges = [range(self.sizes[d]) if d in dims else range(1) for d in range(self.rank)]
        return list(itertools.product(*ranges))

    def along(self, dim, by):
        return tuple(by if d == dim else 0 for d in range(self.rank))

    def flat(self, delta):
        return sum(delta[d] * self.strides[d] for d in range(self.rank))

    def minus(self, one, other):
        return tuple((a - b) % s for a, b, s in zip(one, other, self.sizes))

    def plus(self, one, other):
        return tuple((a + b) % s for a, b, s in zip(one, other, self.sizes))

    def within(self, coords, dims):
        total = 0
        for d in dims:
            total = total * self.sizes[d] + coords[d]
        return total


def layers_kernel(grid, *refs):
    order, stream_hbm, gain_hbm, query_hbm, keyval_hbm, out_hbm, segments = refs[:7]
    result = refs[7]
    (
        stream,
        gains,
        query_all,
        keyval_all,
        out_all,
        sent,
        kept,
        next_kept,
        first_sum,
        w_keyval,
        w_query,
        w_out,
        later_keyval,
        later_query,
        later_out,
        relay_keyval,
        relay_query,
        relay_out,
        part_keyval,
        part_query,
        came_keyval,
        came_query,
        part_square,
        came_square,
        keyvals,
        attended,
        back,
        came_back,
        bias,
        load_sems,
        x_send,
        x_recv,
        w_send,
        w_recv,
        r_send,
        r_recv,
        pk_send,
        pk_recv,
        pq_send,
        pq_recv,
        sq_send,
        sq_recv,
        kv_send,
        kv_recv,
        at_send,
        at_recv,
        b_send,
        b_recv,
    ) = refs[8:]
    sizes = grid.sizes
    ctx_count = math.prod(sizes)
    me = lax.axis_index("ctx")
    section = lax.axis_index("pipe")
    pipe_count = lax.axis_size("pipe")
    coords = [(me // grid.strides[d]) % sizes[d] for d in range(grid.rank)]
    split_count, share_count = len(grid.split), len(grid.share)
    tok_rows, model_width = stream.shape
    half = tok_rows // HALVES
    block = model_width // ctx_count
    wide = block * share_count
    query_width = w_query.shape[-1]
    kv_width = w_keyval.shape[-1]
    head_dim = kv_width // 2
    head_count = query_width // head_dim
    scale = 1.0 / math.sqrt(head_dim)
    stacked = split_count * half

    def moved(delta):
        return [(coords[d] + delta[d]) % sizes[d] for d in range(grid.rank)]

    def place(delta):
        return sum(c * s for c, s in zip(moved(delta), grid.strides))

    def split_slot(delta):
        return grid.within(moved(delta), grid.split_dims)

    def share_slot(delta):
        return grid.within(moved(delta), grid.share_dims)

    def rank_of(half_index, delta):
        where = place(delta)
        return where if half_index == 0 else ctx_count - 1 - where

    def columns(index):
        return pl.ds(pl.multiple_of(index * block, block), block)

    def rows(half_index):
        return pl.ds(half_index * half, half)

    finish = []

    def remote(src, dst, send, recv, ctx, pipe=None):
        device = {"ctx": ctx} if pipe is None else {"ctx": ctx, "pipe": pipe}
        return pltpu.make_async_remote_copy(
            src_ref=src,
            dst_ref=dst,
            send_sem=send,
            recv_sem=recv,
            device_id=device,
            device_id_type=MESH,
        )

    def push(copy, when=None):
        if when is None:
            copy.start()
        else:
            pl.when(when)(copy.start)
        finish.append((copy, when))

    loads = []

    def load(src, dst):
        copy = pltpu.make_async_copy(src, dst, load_sems.at[len(loads)])
        copy.start()
        loads.append(copy)
        return copy

    load_gain = load(gain_hbm, gains)
    load_keyval = load(keyval_hbm, keyval_all)
    load_query = load(query_hbm, query_all)
    load_stream = [load(stream_hbm.at[rows(h)], stream.at[rows(h)]) for h in range(HALVES)]
    load_out = load(out_hbm, out_all)

    keyvals[...] = jnp.zeros_like(keyvals)

    near = sorted(
        set(grid.split + grid.hops + grid.major + grid.minor) - {grid.zero}
    )
    barrier = pltpu.get_barrier_semaphore()
    greeted = 0
    for delta in near:
        pl.semaphore_signal(
            barrier, inc=1, device_id={"ctx": place(delta)}, device_id_type=MESH
        )
        greeted += 1
    for by in sorted({1, pipe_count - 1}):
        for delta in sorted(set([grid.zero] + grid.hops + grid.major)):
            pl.semaphore_signal(
                barrier,
                inc=1,
                device_id={"ctx": place(delta), "pipe": (section + by) % pipe_count},
                device_id_type=MESH,
            )
            greeted += 1

    key_rel = lax.broadcasted_iota(jnp.int32, (half, ctx_count * half), 1)
    row_rel = lax.broadcasted_iota(jnp.int32, (half, ctx_count * half), 0)
    for h in range(HALVES):
        query_rel = row_rel + rank_of(h, grid.zero) * half
        seg = segments[:, h * ctx_count * half : (h + 1) * ctx_count * half].astype(FULL)
        seg = jnp.broadcast_to(seg, (half, ctx_count * half))
        own = jnp.sum(jnp.where(key_rel == query_rel, seg, 0.0), axis=1, keepdims=True)
        bias[h] = jnp.where((key_rel <= query_rel) & (seg == own), 0.0, -1e30)

    factors = {}

    def cast_stream(h):
        load_stream[h].wait()
        squares = jnp.zeros((half, 1), FULL)
        for index, delta in enumerate(grid.split):
            target = kept.at[h, split_slot(grid.zero)] if delta == grid.zero else sent.at[h, index]
            for share in grid.share:
                value = stream[rows(h), columns(place(grid.plus(delta, share)))]
                squares += jnp.sum(value * value, axis=1, keepdims=True)
                target[:, columns(share_slot(share))] = value.astype(LOW)
        factors[0, h] = lax.rsqrt(squares / model_width + 1e-05)

    def send_stream(h):
        for index, delta in enumerate(grid.split):
            if delta != grid.zero:
                seen = grid.split.index(grid.minus(grid.zero, delta))
                push(
                    remote(
                        sent.at[h, index],
                        kept.at[h, split_slot(grid.zero)],
                        x_send.at[h, index],
                        x_recv.at[h, seen],
                        place(delta),
                    )
                )

    def take_stream(h):
        for index, delta in enumerate(grid.split):
            if delta != grid.zero:
                landing = kept.at[h, split_slot(delta)]
                remote(
                    landing, landing, x_send.at[h, index], x_recv.at[h, index], place(delta)
                ).wait_recv()

    wholes = [w_keyval, w_query, w_out]
    laters = [later_keyval, later_query, later_out]
    used = {}

    def fill(kind, tick):
        layer = order[0, tick]
        source = [keyval_all, query_all, out_all][kind]
        value = source[layer]
        if kind < 2:
            level = lax.broadcasted_iota(jnp.int32, gains.shape, 0)
            gain = jnp.where(level == layer, gains[...].astype(FULL), 0.0)
            gain = jnp.sum(gain, axis=0, keepdims=True)
            gain = jnp.transpose(jnp.broadcast_to(gain, (128, block)))
            value = value.astype(FULL)
            value = jnp.concatenate(
                [value[:, c : c + 128] * gain for c in range(0, value.shape[1], 128)], axis=1
            ).astype(LOW)
        if tick == 0:
            wholes[kind][tick, share_slot(grid.zero)] = value
        else:
            laters[kind][...] = value

    def next_send(kind, tick):
        count = used.get((kind, tick), 0)
        used[kind, tick] = count + 1
        return w_send.at[kind, tick, count]

    line = coords[0] * 2 + coords[1] if grid.relayed else 0
    middle = (line + 1) // 2 == 1 if grid.relayed else False
    relays = [relay_keyval, relay_query, relay_out]

    def on_line(where):
        return me + (where - line) * grid.strides[1]

    def begin(kind, tick):
        slot = share_slot(grid.zero)
        landing = wholes[kind].at[tick, slot]
        source = landing if tick == 0 else laters[kind]
        pipe = None if tick == 0 else (section + pipe_count - tick) % pipe_count
        for delta in grid.hops + [grid.zero] * (tick > 0):
            seen = grid.share.index(grid.minus(grid.zero, delta))
            recv = w_recv.at[kind, tick, seen]
            target, where = landing, place(delta)
            if grid.relayed and delta[0]:
                recv = r_recv.at[kind, tick, coords[0]]
                target, where = relays[kind].at[tick, coords[0]], on_line(1 + line % 2)
            push(remote(source, target, next_send(kind, tick), recv, where, pipe))

    def relay_weight(kind, tick):
        if not grid.relayed:
            return
        for origin in range(2):
            landing = relays[kind].at[tick, origin]
            arrival = remote(
                landing,
                landing,
                r_send.at[kind, tick, origin],
                r_recv.at[kind, tick, origin],
                on_line(line - 1 + 2 * (1 - origin)),
            )
            pl.when(middle)(arrival.wait_recv)
            seen = grid.share.index(grid.along(0, 1))
            slot = origin * sizes[2] + coords[2]
            push(
                remote(
                    landing,
                    wholes[kind].at[tick, slot],
                    r_send.at[kind, tick, origin],
                    w_recv.at[kind, tick, seen],
                    on_line(line - 1 + 2 * (1 - origin)),
                ),
                middle,
            )

    def take_weight(kind, tick, phase):
        dims = grid.share_dims
        if phase == 0 and tick:
            landing = wholes[kind].at[tick, share_slot(grid.zero)]
            remote(
                landing,
                landing,
                w_send.at[kind, tick, 0],
                w_recv.at[kind, tick, 0],
                me,
                (section + pipe_count - tick) % pipe_count,
            ).wait_recv()
        for delta in grid.share:
            if delta[dims[phase]] == 0 or any(delta[d] for d in dims[phase + 1 :]):
                continue
            landing = wholes[kind].at[tick, share_slot(delta)]
            remote(
                landing,
                landing,
                w_send.at[kind, tick, 0],
                w_recv.at[kind, tick, grid.share.index(delta)],
                place(grid.along(dims[phase], 1)),
            ).wait_recv()
            for dim in dims[phase + 1 :]:
                for by in range(1, sizes[dim]):
                    hop = grid.along(dim, by)
                    seen = grid.share.index(grid.minus(delta, hop))
                    push(
                        remote(
                            landing,
                            landing,
                            next_send(kind, tick),
                            w_recv.at[kind, tick, seen],
                            place(hop),
                        )
                    )

    phases = range(len(grid.share_dims))
    layered = [kept, next_kept]

    def project(kind, tick, h):
        part = [part_keyval, part_query][kind]
        came = [came_keyval, came_query][kind]
        send, recv = [(pk_send, pk_recv), (pq_send, pq_recv)][kind]
        width = part.shape[-1]
        value = layered[tick][h].reshape(stacked, wide)
        weight = wholes[kind][tick].reshape(wide, width)
        total = jnp.dot(value, weight, preferred_element_type=FULL).astype(LOW)
        part[tick, h] = total.reshape(split_count, half, width)
        for index, delta in enumerate(grid.split):
            if delta != grid.zero:
                seen = grid.split.index(grid.minus(grid.zero, delta))
                push(
                    remote(
                        part.at[tick, h, split_slot(delta)],
                        came.at[tick, h, seen],
                        send.at[tick, h, index],
                        recv.at[tick, h, seen],
                        place(delta),
                    )
                )

    def summed(kind, tick, h):
        part = [part_keyval, part_query][kind]
        came = [came_keyval, came_query][kind]
        send, recv = [(pk_send, pk_recv), (pq_send, pq_recv)][kind]
        total = part[tick, h, split_slot(grid.zero)].astype(FULL)
        for index, delta in enumerate(grid.split):
            if delta != grid.zero:
                landing = came.at[tick, h, index]
                remote(
                    landing,
                    landing,
                    send.at[tick, h, index],
                    recv.at[tick, h, index],
                    place(delta),
                ).wait_recv()
                total += came[tick, h, index].astype(FULL)
        return (total * factors[tick, h]).astype(LOW)

    def send_squares(h, total):
        ones = jnp.ones((8, 128), FULL)
        for index, delta in enumerate(grid.split):
            piece = total[index * half : (index + 1) * half]
            piece = jnp.concatenate([piece] * (128 // half), axis=0)
            part_square[h, index] = lax.dot_general(
                ones,
                piece,
                (((1,), (1,)), ((), ())),
                preferred_element_type=FULL,
                precision=lax.Precision.HIGHEST,
            )
        for index, delta in enumerate(grid.split):
            if delta != grid.zero:
                seen = grid.split.index(grid.minus(grid.zero, delta))
                push(
                    remote(
                        part_square.at[h, split_slot(delta)],
                        came_square.at[h, seen],
                        sq_send.at[h, index],
                        sq_recv.at[h, seen],
                        place(delta),
                    )
                )

    def take_squares(h):
        total = part_square[h, split_slot(grid.zero)]
        for index, delta in enumerate(grid.split):
            if delta != grid.zero:
                landing = came_square.at[h, index]
                remote(
                    landing, landing, sq_send.at[h, index], sq_recv.at[h, index], place(delta)
                ).wait_recv()
                total += came_square[h, index]
        column = jnp.transpose(total)[:half, 0:1]
        factors[1, h] = lax.rsqrt(column / model_width + 1e-05)

    def before(h, delta):
        theirs = grid.within(moved(delta), grid.major_dims)
        ours = grid.within(coords, grid.major_dims)
        return theirs < ours if h == 0 else theirs > ours

    def after(h, delta):
        theirs = grid.within(moved(delta), grid.major_dims)
        ours = grid.within(coords, grid.major_dims)
        return theirs > ours if h == 0 else theirs < ours

    def relay(tick, h, delta, hop, when):
        landing = keyvals.at[tick, h, rank_of(h, delta)]
        seen = grid.minus(delta, hop)
        push(
            remote(
                landing,
                landing,
                kv_send.at[tick, h, grid.flat(grid.plus(delta, hop))],
                kv_recv.at[tick, h, grid.flat(seen)],
                place(hop),
            ),
            when,
        )

    def send_keyvals(tick, h):
        keyvals[tick, h, rank_of(h, grid.zero)] = summed(0, tick, h)
        for delta in grid.major:
            if delta != grid.zero:
                relay(tick, h, grid.zero, delta, after(h, delta))
        for hop in grid.minor:
            if hop != grid.zero:
                relay(tick, h, grid.zero, hop, rank_of(h, hop) > rank_of(h, grid.zero))

    def wait_keyvals(tick, h, delta):
        landing = keyvals.at[tick, h, rank_of(h, delta)]
        remote(
            landing,
            landing,
            kv_send.at[tick, h, 0],
            kv_recv.at[tick, h, grid.flat(delta)],
            place(grid.along(0, 1)),
        ).wait_recv()

    def pass_keyvals(tick, h):
        for delta in grid.major:
            if delta != grid.zero:
                when = before(h, delta)
                pl.when(when)(functools.partial(wait_keyvals, tick, h, delta))
                for hop in grid.minor:
                    if hop != grid.zero:
                        relay(tick, h, delta, hop, when)

    def take_keyvals(tick, h):
        for hop in grid.minor:
            if hop != grid.zero:
                when = rank_of(h, hop) < rank_of(h, grid.zero)
                pl.when(when)(functools.partial(wait_keyvals, tick, h, hop))
        for delta in grid.major:
            if delta != grid.zero:

                @pl.when(before(h, delta))
                def _(delta=delta):
                    for hop in grid.minor:
                        if hop != grid.zero:
                            wait_keyvals(tick, h, grid.plus(delta, hop))

    def attend(tick, h):
        query = summed(1, tick, h)
        query = jnp.concatenate(
            [query[:, i * head_dim : (i + 1) * head_dim] for i in range(head_count)], axis=0
        )
        take_keyvals(tick, h)
        keys = keyvals[tick, h, :, :, :head_dim].reshape(ctx_count * half, head_dim)
        values = keyvals[tick, h, :, :, head_dim:].reshape(ctx_count * half, head_dim)
        scores = lax.dot_general(
            query, keys, (((1,), (1,)), ((), ())), preferred_element_type=FULL
        )
        scores = scores.reshape(head_count, half, ctx_count * half) * scale + bias[h][None]
        probs = jnp.exp(scores - jnp.max(scores, axis=-1, keepdims=True))
        totals = jnp.sum(probs, axis=-1, keepdims=True)
        mixed = jnp.dot(
            probs.astype(LOW).reshape(head_count * half, ctx_count * half),
            values,
            preferred_element_type=FULL,
        ).reshape(head_count, half, head_dim)
        mixed = (mixed / totals).astype(LOW)
        own = attended.at[tick, h, split_slot(grid.zero)]
        for i in range(head_count):
            own[:, i * head_dim : (i + 1) * head_dim] = mixed[i]
        for index, delta in enumerate(grid.split):
            if delta != grid.zero:
                seen = grid.split.index(grid.minus(grid.zero, delta))
                push(
                    remote(
                        own,
                        own,
                        at_send.at[tick, h, index],
                        at_recv.at[tick, h, seen],
                        place(delta),
                    )
                )

    def take_attended(tick, h):
        for index, delta in enumerate(grid.split):
            if delta != grid.zero:
                landing = attended.at[tick, h, split_slot(delta)]
                remote(
                    landing,
                    landing,
                    at_send.at[tick, h, index],
                    at_recv.at[tick, h, index],
                    place(delta),
                ).wait_recv()

    def mix_first(h):
        take_attended(0, h)
        value = attended[0, h].reshape(stacked, query_width)
        squares = jnp.zeros((stacked, 128), FULL)
        for s in range(share_count):
            cols = pl.ds(s * block, block)
            mixed = jnp.dot(value, w_out[0, s], preferred_element_type=FULL)
            first_sum[h, :, :, cols] = mixed.reshape(split_count, half, block)
            following = kept[h, :, :, cols].reshape(stacked, block).astype(FULL) + mixed
            next_kept[h, :, :, cols] = following.astype(LOW).reshape(split_count, half, block)
            following = following * following
            for c in range(0, block, 128):
                squares += following[:, c : c + 128]
        send_squares(h, squares)

    def mix_last(h):
        take_attended(1, h)
        value = attended[1, h].reshape(stacked, query_width)
        for s in range(share_count):
            cols = pl.ds(s * block, block)
            mixed = jnp.dot(value, w_out[1, s], preferred_element_type=FULL)
            mixed = mixed.reshape(split_count, half, block) + first_sum[h, :, :, cols]
            back[h, :, :, cols] = mixed.astype(LOW)
        for index, delta in enumerate(grid.split):
            if delta != grid.zero:
                seen = grid.split.index(grid.minus(grid.zero, delta))
                push(
                    remote(
                        back.at[h, split_slot(delta)],
                        came_back.at[h, seen],
                        b_send.at[h, index],
                        b_recv.at[h, seen],
                        place(delta),
                    )
                )

    def end(h):
        for index, delta in enumerate(grid.split):
            if delta == grid.zero:
                source = back.at[h, split_slot(grid.zero)]
            else:
                source = came_back.at[h, index]
                remote(
                    source, source, b_send.at[h, index], b_recv.at[h, index], place(delta)
                ).wait_recv()
            for share in grid.share:
                cols = columns(place(grid.plus(delta, share)))
                result[rows(h), cols] = source[:, columns(share_slot(share))]

    halves = range(HALVES)
    load_gain.wait()
    load_keyval.wait()
    fill(0, 0)
    load_query.wait()
    fill(1, 0)
    cast_stream(0)
    pl.semaphore_wait(barrier, greeted)
    begin(0, 0)
    begin(1, 0)
    send_stream(0)
    cast_stream(1)
    send_stream(1)
    load_out.wait()
    fill(2, 0)
    relay_weight(0, 0)
    for kind in range(3):
        fill(kind, 1)
    for phase in phases:
        take_weight(0, 0, phase)
    relay_weight(1, 0)
    take_stream(0)
    project(0, 0, 0)
    take_weight(1, 0, 0)
    take_stream(1)
    project(0, 0, 1)
    begin(2, 0)
    for h in halves:
        send_keyvals(0, h)
    for h in halves:
        pass_keyvals(0, h)
    begin(0, 1)
    relay_weight(2, 0)
    for phase in phases[1:]:
        take_weight(1, 0, phase)
    for h in halves:
        project(1, 0, h)
    begin(1, 1)
    relay_weight(0, 1)
    take_weight(2, 0, 0)
    attend(0, 0)
    attend(0, 1)
    relay_weight(1, 1)
    take_weight(0, 1, 0)
    for phase in phases[1:]:
        take_weight(2, 0, phase)
    mix_first(0)
    for phase in phases[1:]:
        take_weight(0, 1, phase)
    project(0, 1, 0)
    mix_first(1)
    project(0, 1, 1)
    begin(2, 1)
    take_weight(1, 1, 0)
    for h in halves:
        take_squares(h)
        send_keyvals(1, h)
    relay_weight(2, 1)
    for h in halves:
        pass_keyvals(1, h)
    take_weight(2, 1, 0)
    for phase in phases[1:]:
        take_weight(1, 1, phase)
    for h in halves:
        project(1, 1, h)
    attend(1, 0)
    attend(1, 1)
    for phase in phases[1:]:
        take_weight(2, 1, phase)
    for h in halves:
        mix_last(h)
    for h in halves:
        end(h)
    for copy, when in finish:
        if when is None:
            copy.wait_send()
        else:
            pl.when(when)(copy.wait_send)


def run_layers(order, stream, gain, query, keyval, out, segments, ctx_count):
    grid = Grid(ctx_count)
    split, share = len(grid.split), len(grid.share)
    tok_rows, model_width = stream.shape
    half = tok_rows // HALVES
    block = model_width // ctx_count
    wide = block * share
    query_width, kv_width = query.shape[-1], keyval.shape[-1]
    vmem = pl.BlockSpec(memory_space=pltpu.VMEM)
    hbm = pl.BlockSpec(memory_space=pl.ANY)
    smem = pl.BlockSpec(memory_space=pltpu.SMEM)
    dma = pltpu.SemaphoreType.DMA
    scratch = [
        pltpu.VMEM(stream.shape, FULL),
        pltpu.VMEM(gain.shape, LOW),
        pltpu.VMEM(query.shape, LOW),
        pltpu.VMEM(keyval.shape, LOW),
        pltpu.VMEM(out.shape, LOW),
        pltpu.VMEM((HALVES, split, half, wide), LOW),
        pltpu.VMEM((HALVES, split, half, wide), LOW),
        pltpu.VMEM((HALVES, split, half, wide), LOW),
        pltpu.VMEM((HALVES, split, half, wide), FULL),
        pltpu.VMEM((TICKS, share, block, kv_width), LOW),
        pltpu.VMEM((TICKS, share, block, query_width), LOW),
        pltpu.VMEM((TICKS, share, query_width, block), LOW),
        pltpu.VMEM((block, kv_width), LOW),
        pltpu.VMEM((block, query_width), LOW),
        pltpu.VMEM((query_width, block), LOW),
        pltpu.VMEM((TICKS, 2, block, kv_width), LOW),
        pltpu.VMEM((TICKS, 2, block, query_width), LOW),
        pltpu.VMEM((TICKS, 2, query_width, block), LOW),
        pltpu.VMEM((TICKS, HALVES, split, half, kv_width), LOW),
        pltpu.VMEM((TICKS, HALVES, split, half, query_width), LOW),
        pltpu.VMEM((TICKS, HALVES, split, half, kv_width), LOW),
        pltpu.VMEM((TICKS, HALVES, split, half, query_width), LOW),
        pltpu.VMEM((HALVES, split, 8, 128), FULL),
        pltpu.VMEM((HALVES, split, 8, 128), FULL),
        pltpu.VMEM((TICKS, HALVES, ctx_count, half, kv_width), LOW),
        pltpu.VMEM((TICKS, HALVES, split, half, query_width), LOW),
        pltpu.VMEM((HALVES, split, half, wide), LOW),
        pltpu.VMEM((HALVES, split, half, wide), LOW),
        pltpu.VMEM((HALVES, half, ctx_count * half), FULL),
        dma((8,)),
        dma((HALVES, split)),
        dma((HALVES, split)),
        dma((3, TICKS, share + 2)),
        dma((3, TICKS, share)),
        dma((3, TICKS, 2)),
        dma((3, TICKS, 2)),
    ]
    scratch += [dma((TICKS, HALVES, split))] * 4
    scratch += [dma((HALVES, split))] * 2
    scratch += [dma((TICKS, HALVES, ctx_count))] * 2
    scratch += [dma((TICKS, HALVES, split))] * 2
    scratch += [dma((HALVES, split))] * 2
    return pl.pallas_call(
        functools.partial(layers_kernel, grid),
        out_shape=jax.ShapeDtypeStruct(stream.shape, LOW),
        in_specs=[smem] + [hbm] * 5 + [vmem],
        out_specs=vmem,
        scratch_shapes=scratch,
        compiler_params=pltpu.CompilerParams(
            collective_id=0, has_side_effects=True, vmem_limit_bytes=56 * 1024 * 1024
        ),
    )(order, stream, gain, query, keyval, out, segments)


def body(activations, norm_gain, w_query, w_keyval, w_out, segment_ids, layer_order):
    ctx_count = lax.axis_size("ctx")
    pipe_count = lax.axis_size("pipe")
    change = run_layers(
        layer_order.reshape(1, TICKS),
        activations[0, 0],
        norm_gain[0],
        w_query[0],
        w_keyval[0],
        w_out[0],
        segment_ids,
        ctx_count,
    )
    state = activations[0, 0] + change.astype(FULL)
    if TICKS % pipe_count:
        pairs = [(i, (i + TICKS) % pipe_count) for i in range(pipe_count)]
        state = lax.ppermute(state, "pipe", pairs)
    return state[None, None]


def solution(mesh):
    in_specs = (
        P("pipe", None, "ctx", None),
        P("pipe", None, "ctx"),
        P("pipe", None, "ctx", None),
        P("pipe", None, "ctx", None),
        P("pipe", None, None, "ctx"),
        P(),
        P(None, "pipe"),
    )
    out_specs = P("pipe", None, "ctx", None)
    return jax.shard_map(body, mesh=mesh, in_specs=in_specs, out_specs=out_specs, check_vma=False)
```
